32 devices in a mesh: groups: 1, seq: 32 (over z, y, x, core).
Axes of the slice: x: 2, y: 2, z: 4, core: 2. Of those that a mesh axis runs over, the one named last changes fastest.
Arguments:
- queries: bfloat16 [8192, 2048], P(('groups', 'seq')), may hold values from -6 to 6
- keys: bfloat16 [8192, 2048], P(('groups', 'seq')), may hold values from -6 to 6
- values: bfloat16 [8192, 2048], P(('groups', 'seq')), may hold values from -6 to 6
- out_weight: bfloat16 [2048, 2048], replicated, may hold values from -0.125 to 0.125
- out_grad: bfloat16 [8192, 2048], P(('groups', 'seq')), may hold values from -6 to 6
Outputs:
- query_grad: bfloat16 [8192, 2048], P(('groups', 'seq'))
- key_grad: bfloat16 [8192, 2048], P(('groups', 'seq'))
- value_grad: bfloat16 [8192, 2048], P(('groups', 'seq'))
- weight_grad: float32 [2048, 2048], P(('groups', 'seq'))
The draws below stay inside these ranges and needn't reach their ends.
All inputs are finite; a program needn't handle non-finite values.
Results may differ from the reference program's by a relative error of at most 0.0033.
Values sent between devices are 32-bit elements; how exact they have to be, the bound alone decides.
No kernel may reach another device: no remote copies, remote signals or barrier semaphores. Data moves between devices by JAX's collectives and lax.ppermute only.
A program may use at most 192 MiB of HBM per device.

```python
import jax
import jax.numpy as jnp
from jax import lax

D = 2048
HEADS = 16
HEAD = 128
TOK_DEV = 256
TOKENS = 8192
HD = 2048


def steps_of(own_key, shape, cuts, least, high):
    gain, own = 1.0, jax.random.fold_in(own_key, 6)
    for axis_at, parts in cuts:
        steps = jnp.exp(jax.random.uniform(jax.random.fold_in(own, axis_at), (parts,), jnp.float32, least / len(cuts), high / len(cuts)))
        gain = gain * jnp.repeat(steps, shape[axis_at] // parts).reshape([-1 if axis == axis_at else 1 for axis in range(len(shape))])
    return gain


def scatter_about(key, dims, spread, limit, shards=(), held_as=jnp.bfloat16):
    factor_of = steps_of(key, dims, shards, -0.22, 0.18) if shards else 1.0
    result = jax.random.normal(key, dims, jnp.float32) * spread * factor_of
    return jnp.minimum(jnp.maximum(result, -limit), limit).astype(held_as)


def setup_inputs(seed: int = 0, part: int = 0) -> dict:
    key_list = jax.random.split(jax.random.key(seed), 6)
    part_keys = jax.random.split(jax.random.fold_in(key_list[5], part), 6)
    queries = scatter_about(part_keys[0], (TOKENS, HD), 1.5, 6.0, ((0, 32),))
    keys = scatter_about(part_keys[1], (TOKENS, HD), 1.5, 6.0, ((0, 32),))
    values = scatter_about(part_keys[2], (TOKENS, HD), 1.0, 6.0, ((0, 32),))
    out_weight = scatter_about(key_list[3], (HD, D), HD ** -0.5, 0.125)
    out_grad = scatter_about(part_keys[4], (TOKENS, D), 1.0, 6.0, ((0, 32),))
    return {"queries": queries, "keys": keys, "values": values, "out_weight": out_weight, "out_grad": out_grad}


def feature(x):
    return jax.nn.elu(x) + 1.0

def attend_block(query_f, key_f, value_f, state, zsum):
    block_len = query_f.shape[0]
    fq = feature(query_f.reshape(block_len, HEADS, HEAD))
    fk = feature(key_f.reshape(block_len, HEADS, HEAD))
    vv = value_f.reshape(block_len, HEADS, HEAD)
    rows = lax.broadcasted_iota(jnp.int32, (block_len, block_len), 0)
    cols = lax.broadcasted_iota(jnp.int32, (block_len, block_len), 1)
    causal = (cols <= rows).astype(jnp.float32)
    scores = jnp.einsum('thd,shd->hts', fq, fk, precision=lax.Precision.HIGHEST) * causal[None]
    numer = jnp.einsum('hts,she->the', scores, vv, precision=lax.Precision.HIGHEST)
    numer = numer + jnp.einsum('thd,hde->the', fq, state, precision=lax.Precision.HIGHEST)
    denom = lax.optimization_barrier(jnp.sum(scores, axis=2)).T + jnp.einsum('thd,hd->th', fq, zsum, precision=lax.Precision.HIGHEST)
    return (numer / denom[:, :, None]).reshape(block_len, HEADS * HEAD)

def forward(query_f, key_f, value_f):
    count = TOKENS // TOK_DEV
    qb = query_f.reshape(count, TOK_DEV, HEADS * HEAD)
    kb = key_f.reshape(count, TOK_DEV, HEADS * HEAD)
    vb = value_f.reshape(count, TOK_DEV, HEADS * HEAD)

    def step(carry, pieces):
        state, zsum = carry
        qp, kp, vp = pieces
        out = attend_block(qp, kp, vp, state, zsum)
        fk = feature(kp.reshape(TOK_DEV, HEADS, HEAD))
        vv = vp.reshape(TOK_DEV, HEADS, HEAD)
        state = state + jnp.einsum('thd,the->hde', fk, vv, precision=lax.Precision.HIGHEST)
        zsum = zsum + lax.optimization_barrier(jnp.sum(fk, axis=0))
        return ((state, zsum), out)
    init = (jnp.zeros((HEADS, HEAD, HEAD), jnp.float32), jnp.zeros((HEADS, HEAD), jnp.float32))
    _, outs = lax.scan(step, init, (qb, kb, vb))
    return outs.reshape(TOKENS, HEADS * HEAD)

def reference(queries, keys, values, out_weight, out_grad):
    query_f = queries.astype(jnp.float32)
    key_f = keys.astype(jnp.float32)
    value_f = values.astype(jnp.float32)
    attended, pullback = jax.vjp(forward, query_f, key_f, value_f)
    rounded = attended.astype(jnp.bfloat16)
    attended_grad = jnp.dot(out_grad, out_weight.T, preferred_element_type=jnp.float32)
    weight_grad = jnp.dot(rounded.T, out_grad, preferred_element_type=jnp.float32)
    query_grad, key_grad, value_grad = pullback(attended_grad)
    return (query_grad.astype(jnp.bfloat16), key_grad.astype(jnp.bfloat16), value_grad.astype(jnp.bfloat16), weight_grad)
```

```python
import functools

import jax
import jax.numpy as jnp
from jax import lax
from jax.experimental import pallas as pl
from jax.experimental.pallas import tpu as pltpu
from jax.sharding import PartitionSpec as P

HEADS = 16
HEAD = 128
HALF = HEAD // 2
ROWS = HEAD + 8
F32 = jnp.float32
BF16 = jnp.bfloat16
NN = (((1,), (0,)), ((), ()))
NT = (((1,), (1,)), ((), ()))
TN = (((0,), (0,)), ((), ()))
PARTS = ((0, 768, (0, 1, 2, 3)), (768, 768, (1, 0, 2, 3)), (1536, 512, (2, 0, 1, 3)))
VMEM_LIMIT = 40 * 1024 * 1024


def split(a):
    high = a.astype(BF16)
    return high, (a - high.astype(F32)).astype(BF16)


def mm(a, b, dims):
    out = lax.dot_general(a[0], b[0], dims, preferred_element_type=F32)
    if len(b) > 1:
        out = out + lax.dot_general(a[0], b[1], dims, preferred_element_type=F32)
    if len(a) > 1:
        out = out + lax.dot_general(a[1], b[0], dims, preferred_element_type=F32)
    return out


def feature(x):
    return jnp.where(x > 0, x + 1.0, jnp.exp(jnp.minimum(x, 0.0)))


def slope(x, f):
    return jnp.where(x > 0, 1.0, f)


def causal(t):
    rows = lax.broadcasted_iota(jnp.int32, (t, t), 0)
    cols = lax.broadcasted_iota(jnp.int32, (t, t), 1)
    return cols <= rows


def each_head(at_ref, one):
    me = at_ref[0]
    core, plane = me % 2, (me // 2) % 4

    def pair(turn, carry):
        place, r = turn // 2, turn % 2
        for side in range(2):
            head = (side ^ core) * 8 + (place ^ plane) * 2 + r
            one(side, place, r, head, pl.ds(pl.multiple_of(head * HEAD, HEAD), HEAD))
        return carry

    lax.fori_loop(0, HEADS // 2, pair, 0)


def put_state(ref, place, r, state, total):
    ref[place, r, :HEAD, :] = state
    first = lax.broadcasted_iota(jnp.int32, (8, HEAD), 0) == 0
    ref[place, r, HEAD:, :] = jnp.where(first, total, 0.0)


def summary_kernel(at_ref, k_ref, v_ref, keep_ref, send_ref):
    def one(side, place, r, head, cols):
        fk = feature(k_ref[:, cols].astype(F32))
        state = mm(split(fk), (v_ref[:, cols],), TN)
        put_state((keep_ref, send_ref)[side], place, r, state, jnp.sum(fk, axis=0, keepdims=True))

    each_head(at_ref, one)


def attend(q, k, v, state, total):
    fq, fk = feature(q.astype(F32)), feature(k.astype(F32))
    fqs, fks = split(fq), split(fk)
    scores = jnp.where(causal(q.shape[0]), mm(fqs, fks, NT), 0.0)
    ss, states = split(scores), split(state)
    numer = mm(ss, (v,), NN) + mm(fqs, states, NN)
    denom = jnp.sum(scores, axis=1, keepdims=True) + jnp.sum(fq * total, axis=1, keepdims=True)
    inv = 1.0 / denom
    return fq, fk, fqs, fks, ss, states, inv, numer * inv


def forward_kernel(at_ref, q_ref, k_ref, v_ref, s0_ref, s1_ref, keep_ref, send_ref):
    me = at_ref[0]
    core, chip = me % 2, me // 2

    def one(side, place, r, head, cols):
        s_ref = (s0_ref, s1_ref)[side]
        state, total = s_ref[place, r, :HEAD, :], s_ref[place, r, HEAD : HEAD + 1, :]
        att = attend(q_ref[:, cols], k_ref[:, cols], v_ref[:, cols], state, total)[-1]
        att = jnp.transpose(att)
        low, high = att[:HALF], att[HALF:]
        keep_ref[head ^ chip] = jnp.where(core == 0, low, high)
        send_ref[head ^ chip] = jnp.where(core == 0, high, low)

    each_head(at_ref, one)


def backward_kernel(
    at_ref, q_ref, k_ref, v_ref, g_ref, s0_ref, s1_ref, qg_ref, dk_ref, dv_ref, keep_ref, send_ref
):
    def one(side, place, r, head, cols):
        s_ref = (s0_ref, s1_ref)[side]
        state, total = s_ref[place, r, :HEAD, :], s_ref[place, r, HEAD : HEAD + 1, :]
        q, v, g = q_ref[:, cols], v_ref[:, cols], g_ref[:, cols]
        fq, fk, fqs, fks, ss, states, inv, att = attend(q, k_ref[:, cols], v, state, total)
        dn = g * inv
        dd = -jnp.sum(g * att, axis=1, keepdims=True) * inv
        dns = split(dn)
        ds = split(jnp.where(causal(q.shape[0]), mm(dns, (v,), NT) + dd, 0.0))
        dfq = mm(ds, fks, NN) + mm(dns, states, NT) + dd * total
        qg_ref[:, cols] = (dfq * slope(q.astype(F32), fq)).astype(BF16)
        dk_ref[:, cols] = mm(ds, fqs, TN)
        dv_ref[:, cols] = mm(ss, dns, TN)
        put_state(
            (keep_ref, send_ref)[side], place, r, mm(fqs, dns, TN), jnp.sum(fq * dd, axis=0, keepdims=True)
        )

    each_head(at_ref, one)


def finish_kernel(at_ref, k_ref, v_ref, dk_ref, dv_ref, s0_ref, s1_ref, kg_ref, vg_ref):
    def one(side, place, r, head, cols):
        s_ref = (s0_ref, s1_ref)[side]
        states, total = split(s_ref[place, r, :HEAD, :]), s_ref[place, r, HEAD : HEAD + 1, :]
        k = k_ref[:, cols].astype(F32)
        fk = feature(k)
        dfk = dk_ref[:, cols] + mm((v_ref[:, cols],), states, NT) + total
        kg_ref[:, cols] = (dfk * slope(k, fk)).astype(BF16)
        vg_ref[:, cols] = (dv_ref[:, cols] + mm(split(fk), states, NN)).astype(BF16)

    each_head(at_ref, one)


def weight_kernel(bit_set, a0_ref, a1_ref, g0_ref, g1_ref, *refs):
    outs, (a_ref, g_ref) = refs[:-2], refs[-2:]
    t = g0_ref.shape[0]
    a_ref[:, :, :t] = a0_ref[...].astype(BF16)
    a_ref[:, :, t:] = a1_ref[...].astype(BF16)
    g_ref[:t, :] = g0_ref[...]
    g_ref[t:, :] = g1_ref[...].astype(BF16)
    for out_ref, (start, width, order) in zip(outs, PARTS, strict=True):
        rels = [rel for rel in range(HEADS) if (rel >> order[0]) & 1 == bit_set]
        lhs = jnp.concatenate([a_ref[rel] for rel in rels], axis=0)
        for at in range(0, width, 256):
            got = jnp.dot(lhs, g_ref[:, start + at : start + at + 256], preferred_element_type=F32)
            out_ref[:, :, at : at + 256] = got.reshape(len(rels), HALF, 256)


def call(kernel, outs, flops, *args, scratch=()):
    moved = sum(a.size * a.dtype.itemsize for a in args) + sum(
        jnp.dtype(o.dtype).itemsize * o.size for o in outs
    )
    specs = [pl.BlockSpec(memory_space=pltpu.SMEM if a.size == 1 else pltpu.VMEM) for a in args]
    return pl.pallas_call(
        kernel,
        out_shape=tuple(outs),
        in_specs=specs,
        out_specs=tuple(pl.BlockSpec(memory_space=pltpu.VMEM) for _ in outs),
        scratch_shapes=list(scratch),
        compiler_params=pltpu.CompilerParams(vmem_limit_bytes=VMEM_LIMIT),
        cost_estimate=pl.CostEstimate(flops=flops, bytes_accessed=moved, transcendentals=0),
    )(*args)


def swap(x, mask):
    n = lax.axis_size("seq")
    return lax.ppermute(x, "seq", [(i, i ^ mask) for i in range(n)])


def entering(keep, send, me, later):
    n = lax.axis_size("seq")
    core, plane = me % 2, (me // 2) % 4
    own, mate = keep, swap(send, 1)
    total = own + mate
    got = [total[0]] + [swap(total[j], 2 * j) for j in range(1, 4)]
    layer = got[0] + got[1] + got[2] + got[3]
    outer = jnp.zeros_like(layer)
    for k in range(1, n // 8):
        pairs = [(i, i + 8 * k) for i in range(n - 8 * k)]
        if later:
            pairs = [(b, a) for a, b in pairs]
        outer = outer + lax.ppermute(layer, "seq", pairs)
    back = []
    for j in range(4):
        x = outer
        for i in range(4):
            if i != j:
                ahead = (plane ^ i) > (plane ^ j) if later else (plane ^ i) < (plane ^ j)
                x = x + jnp.where(ahead, got[i], 0.0)
        back.append(swap(x, 2 * j) if j else x)
    back = jnp.stack(back)
    first = 1 if later else 0
    mine = back + jnp.where(core == first, 0.0, mate)
    other = back + jnp.where(core == first, own, 0.0)
    return mine, swap(other, 1)


def scatter_sum(keeps, sends):
    out = []
    for keep, send, (_, width, order) in zip(keeps, sends, PARTS, strict=True):
        left = sorted(order[1:], reverse=True)
        shape = (2,) * len(left) + (HALF, width)
        got, keep = swap(send, 2 << order[0]).reshape(shape), keep.reshape(shape)
        for bit in order[1:]:
            axis = left.index(bit)
            take = lambda a, i: lax.index_in_dim(a, i, axis, keepdims=False)
            send = take(keep, 1) + take(got, 1)
            keep = take(keep, 0) + take(got, 0)
            got = swap(send, 2 << bit)
            left.remove(bit)
        out.append(keep + got)
    return jnp.concatenate(out, axis=1)


def body(queries, keys, values, out_weight, out_grad):
    t = queries.shape[0]
    unit = 2 * t * t * HEAD * HEADS
    shape = jax.ShapeDtypeStruct
    me = lax.axis_index("seq")
    at = me.astype(jnp.int32).reshape(1)
    state_half = shape((4, 2, ROWS, HEAD), F32)
    wide = shape((t, HEADS * HEAD), F32)
    narrow = shape((t, HEADS * HEAD), BF16)

    grad_mate = swap(out_grad.astype(F32), 1)
    keep, send = call(summary_kernel, [state_half] * 2, unit, at, keys, values)
    s0, s1 = entering(keep, send, me, False)
    attended_grad = lax.dot_general(out_grad, out_weight, NT, preferred_element_type=F32)

    half = shape((HEADS, HALF, t), F32)
    a_keep, a_send = call(forward_kernel, [half] * 2, 7 * unit, at, queries, keys, values, s0, s1)
    a_mate = swap(a_send, 1)
    part_shapes = [shape((HEADS // 2, HALF, width), F32) for _, width, _ in PARTS]
    scratch = (
        pltpu.VMEM((HEADS, HALF, 2 * t), BF16),
        pltpu.VMEM((2 * t, out_grad.shape[1]), BF16),
    )
    weight = lambda bit: call(
        functools.partial(weight_kernel, bit),
        part_shapes,
        4 * unit,
        a_keep,
        a_mate,
        out_grad,
        grad_mate,
        scratch=scratch,
    )
    sends, keeps = weight(1), weight(0)
    query_grad, dk, dv, keep, send = call(
        backward_kernel,
        [narrow, wide, wide, state_half, state_half],
        21 * unit,
        at,
        queries,
        keys,
        values,
        attended_grad,
        s0,
        s1,
    )
    weight_grad = scatter_sum(keeps, sends)
    l0, l1 = entering(keep, send, me, True)
    key_grad, value_grad = call(
        finish_kernel, [narrow, narrow], 3 * unit, at, keys, values, dk, dv, l0, l1
    )
    return (query_grad, key_grad, value_grad, weight_grad)


def solution(mesh):
    placed = (
        P(("groups", "seq"), None),
        P(("groups", "seq"), None),
        P(("groups", "seq"), None),
        P(),
        P(("groups", "seq"), None),
    )
    return jax.shard_map(
        body,
        mesh=mesh,
        in_specs=placed,
        out_specs=(
            P(("groups", "seq"), None),
            P(("groups", "seq"), None),
            P(("groups", "seq"), None),
            P(("groups", "seq"), None),
        ),
        check_vma=False,
    )
```

```python
import functools

import jax
import jax.numpy as jnp
from jax import lax
from jax.experimental import pallas as pl
from jax.experimental.pallas import tpu as pltpu
from jax.sharding import PartitionSpec as P

HEADS = 16
HEAD = 128
HALF = HEAD // 2
ROWS = HEAD + 8
PACK = 2 * HEAD + HEADS
F32 = jnp.float32
BF16 = jnp.bfloat16
NN = (((1,), (0,)), ((), ()))
NT = (((1,), (1,)), ((), ()))
TN = (((0,), (0,)), ((), ()))
PARTS = ((0, 768, (0, 1, 2, 3)), (768, 768, (1, 0, 3, 2)), (1536, 512, (2, 3, 0, 1)))
PAIRS = HEADS // 2
PLACES = PAIRS // 2
VMEM_LIMIT = 12 * 1024 * 1024


def split(a):
    high = a.astype(BF16)
    return high, (a - high.astype(F32)).astype(BF16)


def mm(a, b, dims):
    out = lax.dot_general(a[0], b[0], dims, preferred_element_type=F32)
    if len(b) > 1:
        out = out + lax.dot_general(a[0], b[1], dims, preferred_element_type=F32)
    if len(a) > 1:
        out = out + lax.dot_general(a[1], b[0], dims, preferred_element_type=F32)
    return out


def feature(x):
    return jnp.where(x > 0, x + 1.0, jnp.exp(jnp.minimum(x, 0.0)))


def slope(x, f):
    return jnp.where(x > 0, 1.0, f)


def masked(a, query_dim):
    query = lax.broadcasted_iota(jnp.int32, a.shape, query_dim)
    return jnp.where(lax.broadcasted_iota(jnp.int32, a.shape, 1 - query_dim) <= query, a, 0.0)


def each_head(at_ref, one):
    me = at_ref[0]
    core, plane = me % 2, (me // 2) % 4

    def pair(turn, carry):
        place, r = turn // 2, turn % 2
        for side in range(2):
            head = (side ^ core) * 8 + (place ^ plane) * 2 + r
            one(side, place, r, head, pl.ds(pl.multiple_of(head * HEAD, HEAD), HEAD))
        return carry

    lax.fori_loop(0, HEADS // 2, pair, 0)


def first_of(row):
    return jnp.where(lax.broadcasted_iota(jnp.int32, (8, row.shape[1]), 0) == 0, row, 0.0)


def rows_of(r):
    return slice(r * HEAD, (r + 1) * HEAD)


def times_row(row, b, dims):
    high, low = split(row)
    width = row.shape[1]
    at_top = lax.broadcasted_iota(jnp.int32, (16, width), 0) < 8
    both = jnp.where(at_top, high.astype(F32), low.astype(F32)).astype(BF16)
    out = lax.dot_general(both, b[0], dims, preferred_element_type=F32)
    out = out[:1] + out[8:9]
    if len(b) > 1:
        out = out + lax.dot_general(both, b[1], dims, preferred_element_type=F32)[:1]
    return out


def summary_kernel(at_ref, k_ref, v_ref, keep_ref, send_ref, sum_ref):
    def one(side, place, r, head, cols):
        fk = feature(k_ref[:, cols].astype(F32))
        state = mm((v_ref[:, cols],), split(fk), TN)
        (keep_ref, send_ref)[side][place, pl.ds(r * HEAD, HEAD), :] = state
        sum_ref[pl.ds(head, 1), :] = jnp.sum(fk, axis=0, keepdims=True)

    each_head(at_ref, one)
    for place in range(PLACES):
        keep_ref[place, 2 * HEAD :, :] = sum_ref[...]
        send_ref[place, 2 * HEAD :, :] = sum_ref[...]


def inner_kernel(at_ref, q_ref, k_ref, v_ref, nd_ref):
    def one(side, place, r, head, cols):
        fqs, fks = split(feature(q_ref[:, cols].astype(F32))), split(feature(k_ref[:, cols].astype(F32)))
        scores = masked(mm(fks, fqs, NT), 1)
        nd_ref[head, :HEAD, :] = mm((v_ref[:, cols],), split(scores), TN)
        nd_ref[head, HEAD:, :] = first_of(jnp.sum(scores, axis=0, keepdims=True))

    each_head(at_ref, one)


def grad_kernel(g_ref, w_ref, some_ref, gt_ref, wide_ref):
    got = lax.dot_general(w_ref[...], g_ref[...], NT, preferred_element_type=F32)
    gt_ref[...] = got.reshape(gt_ref.shape)
    wide_ref[...] = some_ref[...].astype(F32)


def attended_grad(out_grad, out_weight):
    t, model = out_grad.shape
    step = model // PAIRS
    return pl.pallas_call(
        grad_kernel,
        grid=(PAIRS,),
        out_shape=(
            jax.ShapeDtypeStruct((HEADS, HEAD, t), F32),
            jax.ShapeDtypeStruct((t, model), F32),
        ),
        in_specs=[
            pl.BlockSpec((t, model), lambda i: (0, 0)),
            pl.BlockSpec((2 * HEAD, model), lambda i: (i, 0)),
            pl.BlockSpec((t, step), lambda i: (0, i)),
        ],
        out_specs=(
            pl.BlockSpec((2, HEAD, t), lambda i: (i, 0, 0)),
            pl.BlockSpec((t, step), lambda i: (0, i)),
        ),
        compiler_params=pltpu.CompilerParams(vmem_limit_bytes=VMEM_LIMIT),
        cost_estimate=pl.CostEstimate(flops=1000, bytes_accessed=1000, transcendentals=0),
    )(out_grad, out_weight, out_grad)


def early_kernel(at_ref, q_ref, nd_ref, gt_ref, z_ref, keep_ref, send_ref, inv_ref):
    def one(side, place, r, head, cols):
        fqs = split(feature(q_ref[:, cols].astype(F32)))
        denom = times_row(z_ref[pl.ds(head, 1), :], fqs, NT)
        inv = 1.0 / (nd_ref[head, HEAD : HEAD + 1, :] + denom)
        inv_ref[head] = first_of(inv)
        state = mm(split(gt_ref[head] * inv), fqs, NN)
        (keep_ref, send_ref)[side][place, pl.ds(r * HEAD, HEAD), :] = state

    each_head(at_ref, one)
    for place in range(PLACES):
        keep_ref[place, 2 * HEAD :, :] = jnp.zeros((HEADS, HEAD), F32)
        send_ref[place, 2 * HEAD :, :] = jnp.zeros((HEADS, HEAD), F32)


def forward_kernel(
    at_ref, q_ref, nd_ref, gt_ref, inv_ref, s0_ref, s1_ref, dkeep_ref, dmate_ref,
    keep_ref, send_ref, dd_ref, t0_ref, t1_ref, t2_ref, t3_ref, dz_ref,
):
    me = at_ref[0]
    core, chip = me % 2, me // 2

    def one(side, place, r, head, cols):
        state = (s0_ref, s1_ref)[side][place, pl.ds(r * HEAD, HEAD), :]
        fqs = split(feature(q_ref[:, cols].astype(F32)))
        inv = inv_ref[head, :1, :]
        att = (nd_ref[head, :HEAD, :] + mm(split(state), fqs, NT)) * inv
        low, high = att[:HALF], att[HALF:]
        keep_ref[head ^ chip] = jnp.where(core == 0, low, high)
        send_ref[head ^ chip] = jnp.where(core == 0, high, low)
        dd = -jnp.sum(gt_ref[head] * att, axis=0, keepdims=True) * inv
        dd_ref[head] = first_of(dd)
        dz_ref[pl.ds(head, 1), :] = times_row(dd, fqs, NN)

    each_head(at_ref, one)
    for j, t_ref in enumerate((t0_ref, t1_ref, t2_ref, t3_ref)):
        t_ref[: 2 * HEAD, :] = dkeep_ref[j, : 2 * HEAD, :] + dmate_ref[j, : 2 * HEAD, :]
        t_ref[2 * HEAD :, :] = dz_ref[...]


def backward_kernel(
    at_ref, q_ref, k_ref, v_ref, gt_ref, inv_ref, dd_ref, z_ref, s0_ref, s1_ref, qg_ref, dk_ref, dv_ref
):
    def one(side, place, r, head, cols):
        state = (s0_ref, s1_ref)[side][place, pl.ds(r * HEAD, HEAD), :]
        q, v = q_ref[:, cols].astype(F32), v_ref[:, cols]
        fq = feature(q)
        fqs, fks = split(fq), split(feature(k_ref[:, cols].astype(F32)))
        ss = split(masked(mm(fks, fqs, NT), 1))
        dn = split(gt_ref[head] * inv_ref[head, :1, :])
        dd = dd_ref[head, :1, :]
        ds = split(masked(mm((v,), dn, NN) + dd, 1))
        z = z_ref[pl.ds(head, 1), :]
        dd_rows, z_rows = (jnp.concatenate([first_of(x)] * 2, axis=0) for x in (dd, z))
        dfq = mm(ds, fks, TN) + mm(dn, split(state), TN) + 0.5 * mm(split(dd_rows), split(z_rows), TN)
        qg_ref[:, cols] = (dfq * slope(q, fq)).astype(BF16)
        dk_ref[:, cols] = mm(ds, fqs, NN)
        dv_ref[:, cols] = mm(ss, dn, NT)

    each_head(at_ref, one)


def finish_kernel(at_ref, k_ref, v_ref, dk_ref, dv_ref, dz_ref, s0_ref, s1_ref, kg_ref, vg_ref):
    def one(side, place, r, head, cols):
        states = split((s0_ref, s1_ref)[side][place, pl.ds(r * HEAD, HEAD), :])
        k = k_ref[:, cols].astype(F32)
        fk = feature(k)
        dfk = dk_ref[:, cols] + mm((v_ref[:, cols],), states, NN) + dz_ref[pl.ds(head, 1), :]
        kg_ref[:, cols] = (dfk * slope(k, fk)).astype(BF16)
        vg_ref[:, cols] = (dv_ref[:, cols] + mm(split(fk), states, NT)).astype(BF16)

    each_head(at_ref, one)


def weight_kernel(bit_set, a0_ref, a1_ref, g0_ref, g1_ref, *refs):
    outs, (a_ref, g_ref) = refs[:-2], refs[-2:]
    t = g0_ref.shape[0]
    a_ref[:, :, :t] = a0_ref[...].astype(BF16)
    a_ref[:, :, t:] = a1_ref[...].astype(BF16)
    g_ref[:t, :] = g0_ref[...]
    g_ref[t:, :] = g1_ref[...].astype(BF16)
    for out_ref, (start, width, order) in zip(outs, PARTS, strict=True):
        rels = [rel for rel in range(HEADS) if (rel >> order[0]) & 1 == bit_set]
        lhs = jnp.concatenate([a_ref[rel] for rel in rels], axis=0)
        for at in range(0, width, 256):
            got = jnp.dot(lhs, g_ref[:, start + at : start + at + 256], preferred_element_type=F32)
            out_ref[:, :, at : at + 256] = got.reshape(len(rels), HALF, 256)


def call(kernel, outs, *args, scratch=()):
    specs = [pl.BlockSpec(memory_space=pltpu.SMEM if a.size == 1 else pltpu.VMEM) for a in args]
    return pl.pallas_call(
        kernel,
        out_shape=tuple(outs),
        in_specs=specs,
        out_specs=tuple(pl.BlockSpec(memory_space=pltpu.VMEM) for _ in outs),
        scratch_shapes=list(scratch),
        compiler_params=pltpu.CompilerParams(vmem_limit_bytes=VMEM_LIMIT),
        cost_estimate=pl.CostEstimate(flops=1000, bytes_accessed=1000, transcendentals=0),
    )(*args)


def swap(x, mask):
    n = lax.axis_size("seq")
    return lax.ppermute(x, "seq", [(i, i ^ mask) for i in range(n)])


def after(first, *arrays):
    arrays, _ = lax.optimization_barrier((arrays, first))
    return arrays if len(arrays) > 1 else arrays[0]


def along(layer, later):
    n = lax.axis_size("seq")
    got = []
    for k in range(1, n // 8):
        pairs = [(i, i + 8 * k) for i in range(n - 8 * k)]
        got.append(lax.ppermute(layer, "seq", [(b, a) for a, b in pairs] if later else pairs))
    return got or [jnp.zeros_like(layer)]


def along_in_turn(layer, first, me, later, beside):
    outer, mask = jnp.zeros_like(layer), 8
    while mask < lax.axis_size("seq"):
        other = after(beside, first) if mask == 8 else swap(layer, mask)
        outer = outer + jnp.where(((me & mask) == 0) == later, other, 0.0)
        layer = layer + other
        mask *= 2
    return outer


def before(got, place, plane, later):
    out = 0.0
    for i, x in enumerate(got):
        if i != place:
            ahead = (plane ^ i) > (plane ^ place) if later else (plane ^ i) < (plane ^ place)
            out = out + jnp.where(ahead, x, 0.0)
    return out


def halves(keep, got, left, bit):
    axis = left.index(bit)
    take = lambda a, i: lax.index_in_dim(a, i, axis, keepdims=False)
    return take(keep, 1) + take(got, 1), take(keep, 0) + take(got, 0)


def body(queries, keys, values, out_weight, out_grad):
    t, model = out_grad.shape
    shape = jax.ShapeDtypeStruct
    me = lax.axis_index("seq")
    core, plane = me % 2, (me // 2) % 4
    at = me.astype(jnp.int32).reshape(1)
    packs = [shape((PLACES, PACK, HEAD), F32)] * 2
    row = shape((HEADS, 8, t), F32)
    sums = shape((HEADS, HEAD), F32)
    wide = shape((t, HEADS * HEAD), F32)
    narrow = shape((t, HEADS * HEAD), BF16)
    places = range(PLACES)
    own_sums = lambda x: x[2 * HEAD :]

    keep, send = call(summary_kernel, packs, at, keys, values, scratch=(pltpu.VMEM((HEADS, HEAD), F32),))
    mate = swap(send, 1)
    gt, grad_wide = attended_grad(out_grad, out_weight)
    (inner,) = call(inner_kernel, [shape((HEADS, ROWS, t), F32)], at, queries, keys, values)
    total = [keep[j] + mate[j] for j in places]
    got = [total[0]] + [swap(total[j], 2 * j) for j in places[1:]]
    layer, inner = lax.optimization_barrier((got[0] + got[1] + got[2] + got[3], inner))
    outer = along(layer, False)
    outer, gt, grad_wide = lax.optimization_barrier((outer, gt, grad_wide))
    outer = sum(outer[1:], outer[0])
    back = [outer + before(got, j, plane, False) for j in places]
    z_in = own_sums(back[0]) + jnp.where(core == 1, own_sums(mate[0]), 0.0)

    z_in = after(back, z_in)
    back = [swap(x, 2 * j) if j else x for j, x in enumerate(back)]
    grad_mate = swap(grad_wide, 1)
    dkeep, dsend, inv = call(early_kernel, packs + [row], at, queries, inner, gt, z_in)
    back, dsend = lax.optimization_barrier((back, dsend))
    dmate = swap(dsend, 1)
    s1 = swap(jnp.stack([x + jnp.where(core == 0, keep[j], 0.0) for j, x in enumerate(back)]), 1)
    s0 = jnp.stack([x + jnp.where(core == 1, mate[j], 0.0) for j, x in enumerate(back)])

    half = shape((HEADS, HALF, t), F32)
    a_keep, a_send, dd, *dtotal = call(
        forward_kernel,
        [half, half, row] + [shape((PACK, HEAD), F32)] * PLACES,
        at,
        queries,
        inner,
        gt,
        inv,
        s0,
        s1,
        dkeep,
        dmate,
        scratch=(pltpu.VMEM((HEADS, HEAD), F32),),
    )
    a_mate = swap(a_send, 1)
    dgot = [dtotal[0]] + [swap(dtotal[j], 2 * j) for j in places[1:]]

    weight = lambda bit: call(
        functools.partial(weight_kernel, bit),
        [shape((HEADS // 2, HALF, width), F32) for _, width, _ in PARTS],
        a_keep,
        a_mate,
        out_grad,
        grad_mate,
        scratch=(pltpu.VMEM((HEADS, HALF, 2 * t), BF16), pltpu.VMEM((2 * t, model), BF16)),
    )
    sends, dgot = lax.optimization_barrier((list(weight(1)), dgot))
    a_mate = after(sends, a_mate)
    keeps = weight(0)
    dlayer = dgot[0] + dgot[1] + dgot[2] + dgot[3]
    gots = [swap(send, 2 << order[0]) for send, (_, _, order) in zip(sends, PARTS, strict=True)]
    dfirst = swap(dlayer, 8)
    queries = after((keeps, dlayer), queries)
    query_grad, dk, dv = call(
        backward_kernel, [narrow, wide, wide], at, queries, keys, values, gt, inv, dd, z_in, s0, s1
    )
    douter = along_in_turn(dlayer, dfirst, me, True, dk)
    gots, douter = lax.optimization_barrier((gots, douter))
    dback = [douter + before(dgot, j, plane, True) for j in places]

    lefts = [sorted(order[1:], reverse=True) for _, _, order in PARTS]
    for turn in range(1, 4):
        sends, kept = [], []
        for keep_part, got, left, (_, width, order) in zip(keeps, gots, lefts, PARTS, strict=True):
            shaped = (2,) * len(left) + (HALF, width)
            send, keep_part = halves(keep_part.reshape(shaped), got.reshape(shaped), left, order[turn])
            sends.append(send)
            kept.append(keep_part)
            left.remove(order[turn])
        keeps = kept
        gots = [swap(send, 2 << order[turn]) for send, (_, _, order) in zip(sends, PARTS, strict=True)]
        if turn == 1:
            dz, dz_part = own_sums(dgot[0]), own_sums(dback[0])
            up = swap(jnp.stack(dback[2:]), 4)
            across = swap(jnp.stack([dback[1], up[1]]), 2)
            dback = [dback[0], across[0], up[0], across[1]]
            gots, dback = lax.optimization_barrier((gots, dback))
        elif turn == 2:
            other = [(x + jnp.where(core == 1, dkeep[j], 0.0))[: 2 * HEAD] for j, x in enumerate(dback)]
            other = [jnp.concatenate([x, dz_part if j == 0 else dz]) for j, x in enumerate(other)]
            l1 = swap(after(sends, jnp.stack(other)), 1)
            l0 = jnp.stack([x + jnp.where(core == 0, dmate[j], 0.0) for j, x in enumerate(dback)])
            gots, l1 = lax.optimization_barrier((gots, l1))
    l0 = after(sends, l0)
    dz_in = dz_part + own_sums(l1[0]) + jnp.where(core == 0, own_sums(l1[1]), 0.0)
    key_grad, value_grad = call(finish_kernel, [narrow, narrow], at, keys, values, dk, dv, dz_in, l0, l1)
    key_grad, gots = lax.optimization_barrier((key_grad, gots))
    parts = [keep_part + got for keep_part, got in zip(keeps, gots, strict=True)]
    weight_grad = jnp.concatenate(parts, axis=1)
    return (query_grad, key_grad, value_grad, weight_grad)


def solution(mesh):
    placed = (
        P(("groups", "seq"), None),
        P(("groups", "seq"), None),
        P(("groups", "seq"), None),
        P(),
        P(("groups", "seq"), None),
    )
    return jax.shard_map(
        body,
        mesh=mesh,
        in_specs=placed,
        out_specs=(
            P(("groups", "seq"), None),
            P(("groups", "seq"), None),
            P(("groups", "seq"), None),
            P(("groups", "seq"), None),
        ),
        check_vma=False,
    )
```

```python
import functools

import jax
import jax.numpy as jnp
from jax import lax
from jax.experimental import pallas as pl
from jax.experimental.pallas import tpu as pltpu
from jax.sharding import PartitionSpec as P

HEADS = 16
HEAD = 128
HALF = HEAD // 2
ROWS = HEAD + 8
PACK = 2 * HEAD + HEADS
F32 = jnp.float32
BF16 = jnp.bfloat16
NN = (((1,), (0,)), ((), ()))
NT = (((1,), (1,)), ((), ()))
TN = (((0,), (0,)), ((), ()))
PARTS = ((0, 768, (0, 1, 2, 3)), (768, 768, (1, 2, 3, 0)), (1536, 512, (2, 0, 1, 3)))
PAIRS = HEADS // 2
PLACES = PAIRS // 2
VMEM_LIMIT = 12 * 1024 * 1024


def split(a):
    high = a.astype(BF16)
    return high, (a - high.astype(F32)).astype(BF16)


def mm(a, b, dims):
    out = lax.dot_general(a[0], b[0], dims, preferred_element_type=F32)
    if len(b) > 1:
        out = out + lax.dot_general(a[0], b[1], dims, preferred_element_type=F32)
    if len(a) > 1:
        out = out + lax.dot_general(a[1], b[0], dims, preferred_element_type=F32)
    return out


def feature(x):
    return jnp.where(x > 0, x + 1.0, jnp.exp(jnp.minimum(x, 0.0)))


def slope(x, f):
    return jnp.where(x > 0, 1.0, f)


def masked(a, query_dim):
    query = lax.broadcasted_iota(jnp.int32, a.shape, query_dim)
    return jnp.where(lax.broadcasted_iota(jnp.int32, a.shape, 1 - query_dim) <= query, a, 0.0)


def each_head(at_ref, one):
    me = at_ref[0]
    core, plane = me % 2, (me // 2) % 4

    def pair(turn, carry):
        place, r = turn // 2, turn % 2
        for side in range(2):
            head = (side ^ core) * 8 + (place ^ plane) * 2 + r
            one(side, place, r, head, pl.ds(pl.multiple_of(head * HEAD, HEAD), HEAD))
        return carry

    lax.fori_loop(0, HEADS // 2, pair, 0)


def first_of(row):
    return jnp.where(lax.broadcasted_iota(jnp.int32, (8, row.shape[1]), 0) == 0, row, 0.0)


def rows_of(r):
    return slice(r * HEAD, (r + 1) * HEAD)


def times_row(row, b, dims):
    high, low = split(row)
    width = row.shape[1]
    at_top = lax.broadcasted_iota(jnp.int32, (16, width), 0) < 8
    both = jnp.where(at_top, high.astype(F32), low.astype(F32)).astype(BF16)
    out = lax.dot_general(both, b[0], dims, preferred_element_type=F32)
    out = out[:1] + out[8:9]
    if len(b) > 1:
        out = out + lax.dot_general(both, b[1], dims, preferred_element_type=F32)[:1]
    return out


def summary_kernel(at_ref, k_ref, v_ref, keep_ref, send_ref, sum_ref):
    def one(side, place, r, head, cols):
        fk = feature(k_ref[:, cols].astype(F32))
        state = mm((v_ref[:, cols],), split(fk), TN)
        (keep_ref, send_ref)[side][place, pl.ds(r * HEAD, HEAD), :] = state
        sum_ref[pl.ds(head, 1), :] = jnp.sum(fk, axis=0, keepdims=True)

    each_head(at_ref, one)
    for place in range(PLACES):
        keep_ref[place, 2 * HEAD :, :] = sum_ref[...]
        send_ref[place, 2 * HEAD :, :] = sum_ref[...]


def inner_kernel(at_ref, q_ref, k_ref, v_ref, nd_ref):
    def one(side, place, r, head, cols):
        fqs, fks = split(feature(q_ref[:, cols].astype(F32))), split(feature(k_ref[:, cols].astype(F32)))
        scores = masked(mm(fks, fqs, NT), 1)
        nd_ref[head, :HEAD, :] = mm((v_ref[:, cols],), split(scores), TN)
        nd_ref[head, HEAD:, :] = first_of(jnp.sum(scores, axis=0, keepdims=True))

    each_head(at_ref, one)


def grad_kernel(g_ref, w_ref, some_ref, gt_ref, wide_ref):
    got = lax.dot_general(w_ref[...], g_ref[...], NT, preferred_element_type=F32)
    gt_ref[...] = got.reshape(gt_ref.shape)
    wide_ref[...] = some_ref[...].astype(F32)


def attended_grad(out_grad, out_weight):
    t, model = out_grad.shape
    step = model // PAIRS
    return pl.pallas_call(
        grad_kernel,
        grid=(PAIRS,),
        out_shape=(
            jax.ShapeDtypeStruct((HEADS, HEAD, t), F32),
            jax.ShapeDtypeStruct((t, model), F32),
        ),
        in_specs=[
            pl.BlockSpec((t, model), lambda i: (0, 0)),
            pl.BlockSpec((2 * HEAD, model), lambda i: (i, 0)),
            pl.BlockSpec((t, step), lambda i: (0, i)),
        ],
        out_specs=(
            pl.BlockSpec((2, HEAD, t), lambda i: (i, 0, 0)),
            pl.BlockSpec((t, step), lambda i: (0, i)),
        ),
        compiler_params=pltpu.CompilerParams(vmem_limit_bytes=VMEM_LIMIT),
        cost_estimate=pl.CostEstimate(flops=1000, bytes_accessed=1000, transcendentals=0),
    )(out_grad, out_weight, out_grad)


def early_kernel(at_ref, q_ref, nd_ref, gt_ref, z_ref, keep_ref, send_ref, inv_ref):
    def one(side, place, r, head, cols):
        fqs = split(feature(q_ref[:, cols].astype(F32)))
        denom = times_row(z_ref[pl.ds(head, 1), :], fqs, NT)
        inv = 1.0 / (nd_ref[head, HEAD : HEAD + 1, :] + denom)
        inv_ref[head] = first_of(inv)
        state = mm(split(gt_ref[head] * inv), fqs, NN)
        (keep_ref, send_ref)[side][place, pl.ds(r * HEAD, HEAD), :] = state

    each_head(at_ref, one)
    for place in range(PLACES):
        keep_ref[place, 2 * HEAD :, :] = jnp.zeros((HEADS, HEAD), F32)
        send_ref[place, 2 * HEAD :, :] = jnp.zeros((HEADS, HEAD), F32)


def attended_of(q_ref, nd_ref, inv_ref, s_ref, place, r, head, cols):
    state = s_ref[place, pl.ds(r * HEAD, HEAD), :]
    fqs = split(feature(q_ref[:, cols].astype(F32)))
    inv = inv_ref[head, :1, :]
    return (nd_ref[head, :HEAD, :] + mm(split(state), fqs, NT)) * inv, inv, fqs


def forward_kernel(at_ref, q_ref, nd_ref, inv_ref, s0_ref, s1_ref, keep_ref, send_ref):
    me = at_ref[0]
    core, chip = me % 2, me // 2

    def one(side, place, r, head, cols):
        att, _, _ = attended_of(q_ref, nd_ref, inv_ref, (s0_ref, s1_ref)[side], place, r, head, cols)
        low, high = att[:HALF], att[HALF:]
        keep_ref[head ^ chip] = jnp.where(core == 0, low, high)
        send_ref[head ^ chip] = jnp.where(core == 0, high, low)

    each_head(at_ref, one)


def denominator_kernel(at_ref, q_ref, nd_ref, gt_ref, inv_ref, s0_ref, s1_ref, dd_ref, dz_ref):
    def one(side, place, r, head, cols):
        att, inv, fqs = attended_of(q_ref, nd_ref, inv_ref, (s0_ref, s1_ref)[side], place, r, head, cols)
        dd = -jnp.sum(gt_ref[head] * att, axis=0, keepdims=True) * inv
        dd_ref[head] = first_of(dd)
        dz_ref[pl.ds(head, 1), :] = times_row(dd, fqs, NN)

    each_head(at_ref, one)


def backward_kernel(
    at_ref, q_ref, k_ref, v_ref, gt_ref, inv_ref, dd_ref, z_ref, s0_ref, s1_ref, qg_ref, dk_ref, dv_ref
):
    def one(side, place, r, head, cols):
        state = (s0_ref, s1_ref)[side][place, pl.ds(r * HEAD, HEAD), :]
        q, v = q_ref[:, cols].astype(F32), v_ref[:, cols]
        fq = feature(q)
        fqs, fks = split(fq), split(feature(k_ref[:, cols].astype(F32)))
        ss = split(masked(mm(fks, fqs, NT), 1))
        dn = split(gt_ref[head] * inv_ref[head, :1, :])
        dd = dd_ref[head, :1, :]
        ds = split(masked(mm((v,), dn, NN) + dd, 1))
        z = z_ref[pl.ds(head, 1), :]
        dd_rows, z_rows = (jnp.concatenate([first_of(x)] * 2, axis=0) for x in (dd, z))
        dfq = mm(ds, fks, TN) + mm(dn, split(state), TN) + 0.5 * mm(split(dd_rows), split(z_rows), TN)
        qg_ref[:, cols] = (dfq * slope(q, fq)).astype(BF16)
        dk_ref[:, cols] = mm(ds, fqs, NN)
        dv_ref[:, cols] = mm(ss, dn, NT)

    each_head(at_ref, one)


def finish_kernel(at_ref, k_ref, v_ref, dk_ref, dv_ref, dz_ref, s0_ref, s1_ref, kg_ref, vg_ref):
    def one(side, place, r, head, cols):
        states = split((s0_ref, s1_ref)[side][place, pl.ds(r * HEAD, HEAD), :])
        k = k_ref[:, cols].astype(F32)
        fk = feature(k)
        dfk = dk_ref[:, cols] + mm((v_ref[:, cols],), states, NN) + dz_ref[pl.ds(head, 1), :]
        kg_ref[:, cols] = (dfk * slope(k, fk)).astype(BF16)
        vg_ref[:, cols] = (dv_ref[:, cols] + mm(split(fk), states, NT)).astype(BF16)

    each_head(at_ref, one)


def weight_kernel(bit_set, a0_ref, a1_ref, g0_ref, g1_ref, *refs):
    outs, (a_ref, g_ref) = refs[:-2], refs[-2:]
    t = g0_ref.shape[0]
    a_ref[:, :, :t] = a0_ref[...].astype(BF16)
    a_ref[:, :, t:] = a1_ref[...].astype(BF16)
    g_ref[:t, :] = g0_ref[...]
    g_ref[t:, :] = g1_ref[...].astype(BF16)
    for out_ref, (start, width, order) in zip(outs, PARTS, strict=True):
        rels = [rel for rel in range(HEADS) if (rel >> order[0]) & 1 == bit_set]
        lhs = jnp.concatenate([a_ref[rel] for rel in rels], axis=0)
        for at in range(0, width, 256):
            got = jnp.dot(lhs, g_ref[:, start + at : start + at + 256], preferred_element_type=F32)
            out_ref[:, :, at : at + 256] = got.reshape(len(rels), HALF, 256)


def call(kernel, outs, *args, scratch=()):
    specs = [pl.BlockSpec(memory_space=pltpu.SMEM if a.size == 1 else pltpu.VMEM) for a in args]
    return pl.pallas_call(
        kernel,
        out_shape=tuple(outs),
        in_specs=specs,
        out_specs=tuple(pl.BlockSpec(memory_space=pltpu.VMEM) for _ in outs),
        scratch_shapes=list(scratch),
        compiler_params=pltpu.CompilerParams(vmem_limit_bytes=VMEM_LIMIT),
        cost_estimate=pl.CostEstimate(flops=1000, bytes_accessed=1000, transcendentals=0),
    )(*args)


def swap(x, mask):
    n = lax.axis_size("seq")
    return lax.ppermute(x, "seq", [(i, i ^ mask) for i in range(n)])


def after(first, *arrays):
    arrays, _ = lax.optimization_barrier((arrays, first))
    return arrays if len(arrays) > 1 else arrays[0]


def along(layer, later):
    n = lax.axis_size("seq")
    got = []
    for k in range(1, n // 8):
        pairs = [(i, i + 8 * k) for i in range(n - 8 * k)]
        got.append(lax.ppermute(layer, "seq", [(b, a) for a, b in pairs] if later else pairs))
    return got or [jnp.zeros_like(layer)]


def along_in_turn(layer, first, me, later, beside):
    outer, mask = jnp.zeros_like(layer), 8
    while mask < lax.axis_size("seq"):
        other = after(beside, first) if mask == 8 else swap(layer, mask)
        outer = outer + jnp.where(((me & mask) == 0) == later, other, 0.0)
        layer = layer + other
        mask *= 2
    return outer


def before(got, place, plane, later):
    out = 0.0
    for i, x in enumerate(got):
        if i != place:
            ahead = (plane ^ i) > (plane ^ place) if later else (plane ^ i) < (plane ^ place)
            out = out + jnp.where(ahead, x, 0.0)
    return out


def half(a, left, bit, which):
    return lax.index_in_dim(a.reshape((2,) * len(left) + a.shape[-2:]), which, left.index(bit), keepdims=False)


def body(queries, keys, values, out_weight, out_grad):
    t, model = out_grad.shape
    shape = jax.ShapeDtypeStruct
    me = lax.axis_index("seq")
    core, plane = me % 2, (me // 2) % 4
    at = me.astype(jnp.int32).reshape(1)
    packs = [shape((PLACES, PACK, HEAD), F32)] * 2
    row = shape((HEADS, 8, t), F32)
    sums = shape((HEADS, HEAD), F32)
    wide = shape((t, HEADS * HEAD), F32)
    narrow = shape((t, HEADS * HEAD), BF16)
    places = range(PLACES)
    own_sums = lambda x: x[2 * HEAD :]
    with_sums = lambda x, tail: jnp.concatenate([x[: 2 * HEAD], tail])

    keep, send = call(summary_kernel, packs, at, keys, values, scratch=(pltpu.VMEM((HEADS, HEAD), F32),))
    mate = swap(send, 1)
    gt, grad_wide = attended_grad(out_grad, out_weight)
    (inner,) = call(inner_kernel, [shape((HEADS, ROWS, t), F32)], at, queries, keys, values)
    total = [keep[j] + mate[j] for j in places]
    got = [total[0]] + [swap(total[j], 2 * j) for j in places[1:]]
    layer, inner = lax.optimization_barrier((got[0] + got[1] + got[2] + got[3], inner))
    outer = along(layer, False)
    outer, gt, grad_wide = lax.optimization_barrier((outer, gt, grad_wide))
    outer = sum(outer[1:], outer[0])
    back = [outer + before(got, j, plane, False) for j in places]
    z_in = own_sums(back[0]) + jnp.where(core == 1, own_sums(mate[0]), 0.0)

    z_in = after(back, z_in)
    back = [swap(x, 2 * j) if j else x for j, x in enumerate(back)]
    grad_mate = swap(grad_wide, 1)
    dkeep, dsend, inv = call(early_kernel, packs + [row], at, queries, inner, gt, z_in)
    back, dsend = lax.optimization_barrier((back, dsend))
    dmate = swap(dsend, 1)
    s1 = swap(jnp.stack([x + jnp.where(core == 0, keep[j], 0.0) for j, x in enumerate(back)]), 1)
    s0 = jnp.stack([x + jnp.where(core == 1, mate[j], 0.0) for j, x in enumerate(back)])

    tall = shape((HEADS, HALF, t), F32)
    dtotal = [dkeep[j] + dmate[j] for j in places]
    dgot = [dtotal[0]] + [swap(dtotal[j], 2 * j) for j in places[1:]]
    a_keep, a_send = call(
        forward_kernel, [tall, tall], at, after(dtotal, queries), inner, inv, s0, s1
    )
    a_mate = swap(a_send, 1)

    weight = lambda bit: call(
        functools.partial(weight_kernel, bit),
        [shape((HEADS // 2, HALF, width), F32) for _, width, _ in PARTS],
        a_keep,
        a_mate,
        out_grad,
        grad_mate,
        scratch=(pltpu.VMEM((HEADS, HALF, 2 * t), BF16), pltpu.VMEM((2 * t, model), BF16)),
    )
    sends, dgot = lax.optimization_barrier((list(weight(1)), dgot))
    a_mate = after(sends, a_mate)
    keeps = weight(0)
    gots = [swap(send, 2 << order[0]) for send, (_, _, order) in zip(sends, PARTS, strict=True)]
    dd, dz = call(
        denominator_kernel, [row, sums], at, after(sends, queries), inner, gt, inv, s0, s1
    )
    dlayer = with_sums(dgot[0] + dgot[1] + dgot[2] + dgot[3], dz)
    dfirst = swap(dlayer, 8)
    queries = after(dlayer, queries)
    query_grad, dk, dv = call(
        backward_kernel, [narrow, wide, wide], at, queries, keys, values, gt, inv, dd, z_in, s0, s1
    )
    douter = along_in_turn(dlayer, dfirst, me, True, dk)
    gots, douter = lax.optimization_barrier((gots, douter))
    dback = [douter + before(dgot, j, plane, True) for j in places]

    behind = own_sums(douter)
    lefts = [sorted(order[1:], reverse=True) for _, _, order in PARTS]
    for turn in range(1, 4):
        bits = [order[turn] for _, _, order in PARTS]
        lists = list(zip(keeps, gots, lefts, bits, strict=True))
        sends = [half(k, left, bit, 1) + half(g, left, bit, 1) for k, g, left, bit in lists]
        keeps, gots = after(sends, keeps, gots)
        lists = list(zip(keeps, gots, lefts, bits, strict=True))
        keeps = [half(k, left, bit, 0) + half(g, left, bit, 0) for k, g, left, bit in lists]
        lefts = [[b for b in left if b != bit] for left, bit in zip(lefts, bits, strict=True)]
        gots = [swap(send, 2 << bit) for send, bit in zip(sends, bits, strict=True)]
        if turn == 2:
            behind, dz_beside = behind + own_sums(across[0]), own_sums(across[1])
            up = jnp.stack([with_sums(dback[2], behind), with_sums(across[1], dz + dz_beside)])
            up = swap(after(sends, up), 4)
            dz_part = behind + own_sums(up[0]) + jnp.where((plane ^ 1) > plane, dz_beside, 0.0)
            dz_part = dz_part + jnp.where((plane ^ 2) > plane, own_sums(up[1]), 0.0)
            dback = [dback[0], across[0], up[0], up[1]]
            other = [x + jnp.where(core == 1, dkeep[j], 0.0) for j, x in enumerate(dback)]
            other = [with_sums(x, dz_part if j == 0 else dz) for j, x in enumerate(other)]
            l1 = swap(jnp.stack(other), 1)
            l0 = jnp.stack([x + jnp.where(core == 0, dmate[j], 0.0) for j, x in enumerate(dback)])
            gots, l0, l1 = lax.optimization_barrier((gots, l0, l1))
        elif turn == 1:
            across = jnp.stack([with_sums(dback[1], behind), with_sums(dback[3], dz)])
            across = swap(after(sends, across), 2)
            gots, across = lax.optimization_barrier((gots, across))
    l0 = after(sends, l0)
    dz_in = dz_part + own_sums(l1[0]) + jnp.where(core == 0, own_sums(l1[1]), 0.0)
    key_grad, value_grad = call(finish_kernel, [narrow, narrow], at, keys, values, dk, dv, dz_in, l0, l1)
    key_grad, gots = lax.optimization_barrier((key_grad, gots))
    parts = [keep_part + got for keep_part, got in zip(keeps, gots, strict=True)]
    weight_grad = jnp.concatenate(parts, axis=1)
    return (query_grad, key_grad, value_grad, weight_grad)


def solution(mesh):
    placed = (
        P(("groups", "seq"), None),
        P(("groups", "seq"), None),
        P(("groups", "seq"), None),
        P(),
        P(("groups", "seq"), None),
    )
    return jax.shard_map(
        body,
        mesh=mesh,
        in_specs=placed,
        out_specs=(
            P(("groups", "seq"), None),
            P(("groups", "seq"), None),
            P(("groups", "seq"), None),
            P(("groups", "seq"), None),
        ),
        check_vma=False,
    )
```

```python
import functools

import jax
import jax.numpy as jnp
from jax import lax
from jax.experimental import pallas as pl
from jax.experimental.pallas import tpu as pltpu
from jax.sharding import PartitionSpec as P

HEADS = 16
HEAD = 128
HALF = HEAD // 2
ROWS = HEAD + 8
PACK = 2 * HEAD + HEADS
F32 = jnp.float32
BF16 = jnp.bfloat16
NN = (((1,), (0,)), ((), ()))
NT = (((1,), (1,)), ((), ()))
TN = (((0,), (0,)), ((), ()))
PARTS = ((0, 768, (1, 2, 3, 0)), (768, 768, (0, 1, 2, 3)), (1536, 512, (2, 0, 1, 3)))
PAIRS = HEADS // 2
PLACES = PAIRS // 2
VMEM_LIMIT = 12 * 1024 * 1024


def split(a):
    high = a.astype(BF16)
    return high, (a - high.astype(F32)).astype(BF16)


def mm(a, b, dims):
    out = lax.dot_general(a[0], b[0], dims, preferred_element_type=F32)
    if len(b) > 1:
        out = out + lax.dot_general(a[0], b[1], dims, preferred_element_type=F32)
    if len(a) > 1:
        out = out + lax.dot_general(a[1], b[0], dims, preferred_element_type=F32)
    return out


def feature(x):
    return jnp.where(x > 0, x + 1.0, jnp.exp(jnp.minimum(x, 0.0)))


def slope(x, f):
    return jnp.where(x > 0, 1.0, f)


def masked(a, query_dim):
    query = lax.broadcasted_iota(jnp.int32, a.shape, query_dim)
    return jnp.where(lax.broadcasted_iota(jnp.int32, a.shape, 1 - query_dim) <= query, a, 0.0)


def each_head(at_ref, one):
    me = at_ref[0]
    core, plane = me % 2, (me // 2) % 4

    def pair(turn, carry):
        place, r = turn // 2, turn % 2
        for side in range(2):
            head = (side ^ core) * 8 + (place ^ plane) * 2 + r
            one(side, place, r, head, pl.ds(pl.multiple_of(head * HEAD, HEAD), HEAD))
        return carry

    lax.fori_loop(0, HEADS // 2, pair, 0)


def first_of(row):
    return jnp.where(lax.broadcasted_iota(jnp.int32, (8, row.shape[1]), 0) == 0, row, 0.0)


def rows_of(r):
    return slice(r * HEAD, (r + 1) * HEAD)


def times_row(row, b, dims):
    high, low = split(row)
    width = row.shape[1]
    at_top = lax.broadcasted_iota(jnp.int32, (16, width), 0) < 8
    both = jnp.where(at_top, high.astype(F32), low.astype(F32)).astype(BF16)
    out = lax.dot_general(both, b[0], dims, preferred_element_type=F32)
    out = out[:1] + out[8:9]
    if len(b) > 1:
        out = out + lax.dot_general(both, b[1], dims, preferred_element_type=F32)[:1]
    return out


def summary_kernel(at_ref, k_ref, v_ref, keep_ref, send_ref, sum_ref):
    def one(side, place, r, head, cols):
        fk = feature(k_ref[:, cols].astype(F32))
        state = mm((v_ref[:, cols],), split(fk), TN)
        (keep_ref, send_ref)[side][place, pl.ds(r * HEAD, HEAD), :] = state
        sum_ref[pl.ds(head, 1), :] = jnp.sum(fk, axis=0, keepdims=True)

    each_head(at_ref, one)
    for place in range(PLACES):
        keep_ref[place, 2 * HEAD :, :] = sum_ref[...]
        send_ref[place, 2 * HEAD :, :] = sum_ref[...]


def inner_kernel(at_ref, q_ref, k_ref, v_ref, nd_ref):
    def one(side, place, r, head, cols):
        fqs, fks = split(feature(q_ref[:, cols].astype(F32))), split(feature(k_ref[:, cols].astype(F32)))
        scores = masked(mm(fks, fqs, NT), 1)
        nd_ref[head, :HEAD, :] = mm((v_ref[:, cols],), split(scores), TN)
        nd_ref[head, HEAD:, :] = first_of(jnp.sum(scores, axis=0, keepdims=True))

    each_head(at_ref, one)


def grad_kernel(g_ref, w_ref, own_ref, mate_ref, gt_ref, both_ref):
    got = lax.dot_general(w_ref[...], g_ref[...], NT, preferred_element_type=F32)
    gt_ref[...] = got.reshape(gt_ref.shape)
    t = g_ref.shape[0]
    both_ref[:t, :] = own_ref[...]
    both_ref[t:, :] = mate_ref[...].astype(BF16)


def attended_grad(out_grad, out_weight, grad_mate):
    t, model = out_grad.shape
    some = 4
    steps = HEADS // some
    columns = lambda rows: pl.BlockSpec((rows, model // steps), lambda i: (0, i))
    return pl.pallas_call(
        grad_kernel,
        grid=(steps,),
        out_shape=(
            jax.ShapeDtypeStruct((HEADS, HEAD, t), F32),
            jax.ShapeDtypeStruct((2 * t, model), BF16),
        ),
        in_specs=[
            pl.BlockSpec((t, model), lambda i: (0, 0)),
            pl.BlockSpec((some * HEAD, model), lambda i: (i, 0)),
            columns(t),
            columns(t),
        ],
        out_specs=(pl.BlockSpec((some, HEAD, t), lambda i: (i, 0, 0)), columns(2 * t)),
        compiler_params=pltpu.CompilerParams(vmem_limit_bytes=VMEM_LIMIT),
        cost_estimate=pl.CostEstimate(flops=1000, bytes_accessed=1000, transcendentals=0),
    )(out_grad, out_weight, out_grad, grad_mate)


def back_kernel(at_ref, mate_ref, *refs):
    me = at_ref[0]
    core, plane = me % 2, (me // 2) % 4
    got, outer, outs = refs[:PLACES], refs[PLACES : -PLACES - 1], refs[-PLACES - 1 :]
    total = outer[0][...]
    for ref in outer[1:]:
        total = total + ref[...]
    for j in range(PLACES):
        x = total
        for i in range(PLACES):
            if i != j:
                x = x + jnp.where((plane ^ i) < (plane ^ j), got[i][...], 0.0)
        outs[j][...] = x
        if j == 0:
            outs[-1][...] = x[2 * HEAD :] + jnp.where(core == 1, mate_ref[0, 2 * HEAD :, :], 0.0)


def early_kernel(at_ref, q_ref, nd_ref, gt_ref, z_ref, keep_ref, send_ref, inv_ref):
    def one(side, place, r, head, cols):
        fqs = split(feature(q_ref[:, cols].astype(F32)))
        denom = times_row(z_ref[pl.ds(head, 1), :], fqs, NT)
        inv = 1.0 / (nd_ref[head, HEAD : HEAD + 1, :] + denom)
        inv_ref[head] = first_of(inv)
        state = mm(split(gt_ref[head] * inv), fqs, NN)
        (keep_ref, send_ref)[side][place, pl.ds(r * HEAD, HEAD), :] = state

    each_head(at_ref, one)
    for place in range(PLACES):
        keep_ref[place, 2 * HEAD :, :] = jnp.zeros((HEADS, HEAD), F32)
        send_ref[place, 2 * HEAD :, :] = jnp.zeros((HEADS, HEAD), F32)


def attended_of(q_ref, nd_ref, inv_ref, s_ref, place, r, head, cols):
    state = s_ref[place, pl.ds(r * HEAD, HEAD), :]
    fqs = split(feature(q_ref[:, cols].astype(F32)))
    inv = inv_ref[head, :1, :]
    return (nd_ref[head, :HEAD, :] + mm(split(state), fqs, NT)) * inv, inv, fqs


def forward_kernel(at_ref, q_ref, nd_ref, inv_ref, s0_ref, s1_ref, keep_ref, send_ref):
    me = at_ref[0]
    core, chip = me % 2, me // 2

    def one(side, place, r, head, cols):
        att, _, _ = attended_of(q_ref, nd_ref, inv_ref, (s0_ref, s1_ref)[side], place, r, head, cols)
        low, high = att[:HALF], att[HALF:]
        keep_ref[head ^ chip] = jnp.where(core == 0, low, high)
        send_ref[head ^ chip] = jnp.where(core == 0, high, low)

    each_head(at_ref, one)


def denominator_kernel(at_ref, q_ref, nd_ref, gt_ref, inv_ref, s0_ref, s1_ref, dd_ref, dz_ref):
    def one(side, place, r, head, cols):
        att, inv, fqs = attended_of(q_ref, nd_ref, inv_ref, (s0_ref, s1_ref)[side], place, r, head, cols)
        dd = -jnp.sum(gt_ref[head] * att, axis=0, keepdims=True) * inv
        dd_ref[head] = first_of(dd)
        dz_ref[pl.ds(head, 1), :] = times_row(dd, fqs, NN)

    each_head(at_ref, one)


def backward_kernel(
    at_ref, q_ref, k_ref, v_ref, gt_ref, inv_ref, dd_ref, z_ref, s0_ref, s1_ref, qg_ref, dk_ref, dv_ref
):
    def one(side, place, r, head, cols):
        state = (s0_ref, s1_ref)[side][place, pl.ds(r * HEAD, HEAD), :]
        q, v = q_ref[:, cols].astype(F32), v_ref[:, cols]
        fq = feature(q)
        fqs, fks = split(fq), split(feature(k_ref[:, cols].astype(F32)))
        ss = split(masked(mm(fks, fqs, NT), 1))
        dn = split(gt_ref[head] * inv_ref[head, :1, :])
        dd = dd_ref[head, :1, :]
        ds = split(masked(mm((v,), dn, NN) + dd, 1))
        z = z_ref[pl.ds(head, 1), :]
        dd_rows, z_rows = (jnp.concatenate([first_of(x)] * 2, axis=0) for x in (dd, z))
        dfq = mm(ds, fks, TN) + mm(dn, split(state), TN) + 0.5 * mm(split(dd_rows), split(z_rows), TN)
        qg_ref[:, cols] = (dfq * slope(q, fq)).astype(BF16)
        dk_ref[:, cols] = mm(ds, fqs, NN)
        dv_ref[:, cols] = mm(ss, dn, NT)

    each_head(at_ref, one)


def finish_kernel(at_ref, k_ref, v_ref, dk_ref, dv_ref, dz_ref, s0_ref, s1_ref, kg_ref, vg_ref):
    def one(side, place, r, head, cols):
        states = split((s0_ref, s1_ref)[side][place, pl.ds(r * HEAD, HEAD), :])
        k = k_ref[:, cols].astype(F32)
        fk = feature(k)
        dfk = dk_ref[:, cols] + mm((v_ref[:, cols],), states, NN) + dz_ref[pl.ds(head, 1), :]
        kg_ref[:, cols] = (dfk * slope(k, fk)).astype(BF16)
        vg_ref[:, cols] = (dv_ref[:, cols] + mm(split(fk), states, NT)).astype(BF16)

    each_head(at_ref, one)


def weight_kernel(bit_set, a0_ref, a1_ref, g_ref, *refs):
    outs, a_ref = refs[:-1], refs[-1]
    t = a0_ref.shape[2]
    a_ref[:, :, :t] = a0_ref[...].astype(BF16)
    a_ref[:, :, t:] = a1_ref[...].astype(BF16)
    for out_ref, (start, width, order) in zip(outs, PARTS, strict=True):
        rels = [rel for rel in range(HEADS) if (rel >> order[0]) & 1 == bit_set]
        lhs = jnp.concatenate([a_ref[rel] for rel in rels], axis=0)
        for at in range(0, width, 256):
            got = jnp.dot(lhs, g_ref[:, start + at : start + at + 256], preferred_element_type=F32)
            out_ref[:, :, at : at + 256] = got.reshape(len(rels), HALF, 256)


def call(kernel, outs, *args, scratch=()):
    specs = [pl.BlockSpec(memory_space=pltpu.SMEM if a.size == 1 else pltpu.VMEM) for a in args]
    return pl.pallas_call(
        kernel,
        out_shape=tuple(outs),
        in_specs=specs,
        out_specs=tuple(pl.BlockSpec(memory_space=pltpu.VMEM) for _ in outs),
        scratch_shapes=list(scratch),
        compiler_params=pltpu.CompilerParams(vmem_limit_bytes=VMEM_LIMIT),
        cost_estimate=pl.CostEstimate(flops=1000, bytes_accessed=1000, transcendentals=0),
    )(*args)


def swap(x, mask):
    n = lax.axis_size("seq")
    return lax.ppermute(x, "seq", [(i, i ^ mask) for i in range(n)])


def after(first, *arrays):
    arrays, _ = lax.optimization_barrier((arrays, first))
    return arrays if len(arrays) > 1 else arrays[0]


def along(layer, later):
    n = lax.axis_size("seq")
    got = []
    for k in range(1, n // 8):
        pairs = [(i, i + 8 * k) for i in range(n - 8 * k)]
        got.append(lax.ppermute(layer, "seq", [(b, a) for a, b in pairs] if later else pairs))
    return got or [jnp.zeros_like(layer)]


def along_in_turn(layer, first, me, later, beside):
    outer, mask = jnp.zeros_like(layer), 8
    while mask < lax.axis_size("seq"):
        other = after(beside, first) if mask == 8 else swap(layer, mask)
        outer = outer + jnp.where(((me & mask) == 0) == later, other, 0.0)
        layer = layer + other
        mask *= 2
    return outer


def before(got, place, plane, later):
    out = 0.0
    for i, x in enumerate(got):
        if i != place:
            ahead = (plane ^ i) > (plane ^ place) if later else (plane ^ i) < (plane ^ place)
            out = out + jnp.where(ahead, x, 0.0)
    return out


def half(a, left, bit, which):
    return lax.index_in_dim(a.reshape((2,) * len(left) + a.shape[-2:]), which, left.index(bit), keepdims=False)


def one_turn(keep, got, left, bit):
    send = half(keep, left, bit, 1) + half(got, left, bit, 1)
    keep, got = after(send, keep, got)
    return half(keep, left, bit, 0) + half(got, left, bit, 0), swap(send, 2 << bit)


def sums_of(order, keep, got):
    left = sorted(order[1:], reverse=True)
    for bit in order[1:]:
        keep, got = one_turn(keep, got, left, bit)
        left = [b for b in left if b != bit]
        got = after((yield keep, got), got)


def body(queries, keys, values, out_weight, out_grad):
    t, model = out_grad.shape
    shape = jax.ShapeDtypeStruct
    me = lax.axis_index("seq")
    core, plane = me % 2, (me // 2) % 4
    at = me.astype(jnp.int32).reshape(1)
    packs = [shape((PLACES, PACK, HEAD), F32)] * 2
    row = shape((HEADS, 8, t), F32)
    sums = shape((HEADS, HEAD), F32)
    wide = shape((t, HEADS * HEAD), F32)
    narrow = shape((t, HEADS * HEAD), BF16)
    places = range(PLACES)
    own_sums = lambda x: x[2 * HEAD :]
    with_sums = lambda x, tail: jnp.concatenate([x[: 2 * HEAD], tail])

    keep, send = call(summary_kernel, packs, at, keys, values, scratch=(pltpu.VMEM((HEADS, HEAD), F32),))
    mate = swap(send, 1)
    grad_mate = swap(out_grad.astype(F32), 1)
    (inner,) = call(
        inner_kernel, [shape((HEADS, ROWS, t), F32)], at, queries, keys, values
    )
    total = [keep[j] + mate[j] for j in places]
    got = [total[0]] + [swap(total[j], 2 * j) for j in places[1:]]
    layer, inner, grad_mate = lax.optimization_barrier((got[0] + got[1] + got[2] + got[3], inner, grad_mate))
    outer = along(layer, False)
    gt, grads = attended_grad(out_grad, out_weight, grad_mate)
    outer, gt, grads = lax.optimization_barrier((outer, gt, grads))
    pack = shape((PACK, HEAD), F32)
    *back, z_in = call(back_kernel, [pack] * PLACES + [sums], at, mate, *got, *outer)

    back = [swap(x, 2 * j) if j else x for j, x in enumerate(back)]
    dkeep, dsend, inv = call(early_kernel, packs + [row], at, queries, inner, gt, z_in)
    back, dsend = lax.optimization_barrier((back, dsend))
    dmate = swap(dsend, 1)
    s1 = swap(jnp.stack([x + jnp.where(core == 0, keep[j], 0.0) for j, x in enumerate(back)]), 1)
    s0 = jnp.stack([x + jnp.where(core == 1, mate[j], 0.0) for j, x in enumerate(back)])

    tall = shape((HEADS, HALF, t), F32)
    dtotal = [dkeep[j] + dmate[j] for j in places]
    dgot = [dtotal[0]] + [swap(dtotal[j], 2 * j) for j in places[1:]]
    a_keep, a_send = call(
        forward_kernel, [tall, tall], at, after(dtotal, queries), inner, inv, s0, s1
    )
    a_mate = swap(a_send, 1)

    weight = lambda bit: call(
        functools.partial(weight_kernel, bit),
        [shape((HEADS // 2, HALF, width), F32) for _, width, _ in PARTS],
        a_keep,
        a_mate,
        grads,
        scratch=(pltpu.VMEM((HEADS, HALF, 2 * t), BF16),),
    )
    sends, dgot = lax.optimization_barrier((list(weight(1)), dgot))
    a_mate = after(sends, a_mate)
    keeps = weight(0)
    gots = [swap(send, 2 << order[0]) for send, (_, _, order) in zip(sends, PARTS, strict=True)]
    dd, dz = call(
        denominator_kernel, [row, sums], at, after(sends, queries), inner, gt, inv, s0, s1
    )
    dlayer = with_sums(dgot[0] + dgot[1] + dgot[2] + dgot[3], dz)
    dfirst = swap(dlayer, 8)
    queries = after(dlayer, queries)
    query_grad, dk, dv = call(
        backward_kernel, [narrow, wide, wide], at, queries, keys, values, gt, inv, dd, z_in, s0, s1
    )
    douter = along_in_turn(dlayer, dfirst, me, True, dk)
    free = sums_of(PARTS[-1][2], keeps[-1], after(dk, gots[-1]))
    next(free)
    keeps, gots = keeps[:-1], gots[:-1]
    gots, douter = lax.optimization_barrier((gots, douter))
    dback = [douter + before(dgot, j, plane, True) for j in places]

    behind = own_sums(douter)
    lefts = [sorted(order[1:], reverse=True) for _, _, order in PARTS[:-1]]
    for turn in (1, 2):
        bits = [order[turn] for _, _, order in PARTS[:-1]]
        lists = list(zip(keeps, gots, lefts, bits, strict=True))
        sends = [half(k, left, bit, 1) + half(g, left, bit, 1) for k, g, left, bit in lists]
        keeps, gots = after(sends, keeps, gots)
        lists = list(zip(keeps, gots, lefts, bits, strict=True))
        keeps = [half(k, left, bit, 0) + half(g, left, bit, 0) for k, g, left, bit in lists]
        lefts = [[b for b in left if b != bit] for left, bit in zip(lefts, bits, strict=True)]
        gots = [swap(send, 2 << bit) for send, bit in zip(sends, bits, strict=True)]
        if turn == 2:
            free.send(sends)
            behind, dz_beside = behind + own_sums(across[0]), own_sums(across[1])
            up = jnp.stack([with_sums(dback[2], behind), with_sums(across[1], dz + dz_beside)])
            up = swap(after(sends, up), 4)
            dz_part = behind + own_sums(up[0]) + jnp.where((plane ^ 1) > plane, dz_beside, 0.0)
            dz_part = dz_part + jnp.where((plane ^ 2) > plane, own_sums(up[1]), 0.0)
            dback = [dback[0], across[0], up[0], up[1]]
            other = [x + jnp.where(core == 1, dkeep[j], 0.0) for j, x in enumerate(dback)]
            other = [with_sums(x, dz_part if j == 0 else dz) for j, x in enumerate(other)]
            other = jnp.stack(other)
            l1 = swap(other, 1)
            l0 = jnp.stack([x + jnp.where(core == 0, dmate[j], 0.0) for j, x in enumerate(dback)])
            result = free.send(other)
            ends = [one_turn(keeps[1], after(other, gots[1]), lefts[1], PARTS[1][2][3])]
        elif turn == 1:
            across = jnp.stack([with_sums(dback[1], behind), with_sums(dback[3], dz)])
            across = swap(after(sends, across), 2)
            gots, across = lax.optimization_barrier((gots, across))
    dz_in = dz_part + own_sums(l1[0]) + jnp.where(core == 0, own_sums(l1[1]), 0.0)
    key_grad, value_grad = call(finish_kernel, [narrow, narrow], at, keys, values, dk, dv, dz_in, l0, l1)
    ends.insert(0, one_turn(keeps[0], after(key_grad, gots[0]), lefts[0], PARTS[0][2][3]))
    key_grad, ends = lax.optimization_barrier((key_grad, [*ends, result]))
    parts = [keep_part + got for keep_part, got in ends]
    weight_grad = jnp.concatenate(parts, axis=1)
    return (query_grad, key_grad, value_grad, weight_grad)


def solution(mesh):
    placed = (
        P(("groups", "seq"), None),
        P(("groups", "seq"), None),
        P(("groups", "seq"), None),
        P(),
        P(("groups", "seq"), None),
    )
    return jax.shard_map(
        body,
        mesh=mesh,
        in_specs=placed,
        out_specs=(
            P(("groups", "seq"), None),
            P(("groups", "seq"), None),
            P(("groups", "seq"), None),
            P(("groups", "seq"), None),
        ),
        check_vma=False,
    )
```

```python
import functools

import jax
import jax.numpy as jnp
from jax import lax
from jax.experimental import pallas as pl
from jax.experimental.pallas import tpu as pltpu
from jax.sharding import PartitionSpec as P

HEADS = 16
HEAD = 128
HALF = HEAD // 2
ROWS = HEAD + 8
PACK = 2 * HEAD + HEADS
F32 = jnp.float32
BF16 = jnp.bfloat16
NN = (((1,), (0,)), ((), ()))
NT = (((1,), (1,)), ((), ()))
TN = (((0,), (0,)), ((), ()))
PARTS = ((0, 768, (1, 2, 3, 0)), (768, 768, (0, 1, 2, 3)), (1536, 512, (2, 0, 1, 3)))
PAIRS = HEADS // 2
PLACES = PAIRS // 2
VMEM_LIMIT = 12 * 1024 * 1024


def split(a):
    high = a.astype(BF16)
    return high, (a - high.astype(F32)).astype(BF16)


def mm(a, b, dims):
    out = lax.dot_general(a[0], b[0], dims, preferred_element_type=F32)
    if len(b) > 1:
        out = out + lax.dot_general(a[0], b[1], dims, preferred_element_type=F32)
    if len(a) > 1:
        out = out + lax.dot_general(a[1], b[0], dims, preferred_element_type=F32)
    return out


def feature(x):
    return jnp.where(x > 0, x + 1.0, jnp.exp(jnp.minimum(x, 0.0)))


def slope(x, f):
    return jnp.where(x > 0, 1.0, f)


def masked(a, query_dim):
    query = lax.broadcasted_iota(jnp.int32, a.shape, query_dim)
    return jnp.where(lax.broadcasted_iota(jnp.int32, a.shape, 1 - query_dim) <= query, a, 0.0)


def each_head(at_ref, one):
    me = at_ref[0]
    core, plane = me % 2, (me // 2) % 4

    def pair(turn, carry):
        place, r = turn // 2, turn % 2
        for side in range(2):
            head = (side ^ core) * 8 + (place ^ plane) * 2 + r
            one(side, place, r, head, pl.ds(pl.multiple_of(head * HEAD, HEAD), HEAD))
        return carry

    lax.fori_loop(0, HEADS // 2, pair, 0)


def first_of(row):
    return jnp.where(lax.broadcasted_iota(jnp.int32, (8, row.shape[1]), 0) == 0, row, 0.0)


def rows_of(r):
    return slice(r * HEAD, (r + 1) * HEAD)


def times_row(row, b, dims):
    high, low = split(row)
    width = row.shape[1]
    at_top = lax.broadcasted_iota(jnp.int32, (16, width), 0) < 8
    both = jnp.where(at_top, high.astype(F32), low.astype(F32)).astype(BF16)
    out = lax.dot_general(both, b[0], dims, preferred_element_type=F32)
    out = out[:1] + out[8:9]
    if len(b) > 1:
        out = out + lax.dot_general(both, b[1], dims, preferred_element_type=F32)[:1]
    return out


def summary_kernel(at_ref, k_ref, v_ref, keep_ref, send_ref, sum_ref):
    def one(side, place, r, head, cols):
        fk = feature(k_ref[:, cols].astype(F32))
        state = mm((v_ref[:, cols],), split(fk), TN)
        (keep_ref, send_ref)[side][place, pl.ds(r * HEAD, HEAD), :] = state
        sum_ref[pl.ds(head, 1), :] = jnp.sum(fk, axis=0, keepdims=True)

    each_head(at_ref, one)
    for place in range(PLACES):
        keep_ref[place, 2 * HEAD :, :] = sum_ref[...]
        send_ref[place, 2 * HEAD :, :] = sum_ref[...]


def inner_kernel(at_ref, q_ref, k_ref, v_ref, nd_ref):
    def one(side, place, r, head, cols):
        fqs, fks = split(feature(q_ref[:, cols].astype(F32))), split(feature(k_ref[:, cols].astype(F32)))
        scores = masked(mm(fks, fqs, NT), 1)
        nd_ref[head, :HEAD, :] = mm((v_ref[:, cols],), split(scores), TN)
        nd_ref[head, HEAD:, :] = first_of(jnp.sum(scores, axis=0, keepdims=True))

    each_head(at_ref, one)


def grad_kernel(g_ref, w_ref, own_ref, mate_ref, gt_ref, both_ref):
    got = lax.dot_general(w_ref[...], g_ref[...], NT, preferred_element_type=F32)
    gt_ref[...] = got.reshape(gt_ref.shape)
    t = g_ref.shape[0]
    both_ref[:t, :] = own_ref[...]
    both_ref[t:, :] = mate_ref[...].astype(BF16)


def attended_grad(out_grad, out_weight, grad_mate):
    t, model = out_grad.shape
    some = 4
    steps = HEADS // some
    columns = lambda rows: pl.BlockSpec((rows, model // steps), lambda i: (0, i))
    return pl.pallas_call(
        grad_kernel,
        grid=(steps,),
        out_shape=(
            jax.ShapeDtypeStruct((HEADS, HEAD, t), F32),
            jax.ShapeDtypeStruct((2 * t, model), BF16),
        ),
        in_specs=[
            pl.BlockSpec((t, model), lambda i: (0, 0)),
            pl.BlockSpec((some * HEAD, model), lambda i: (i, 0)),
            columns(t),
            columns(t),
        ],
        out_specs=(pl.BlockSpec((some, HEAD, t), lambda i: (i, 0, 0)), columns(2 * t)),
        compiler_params=pltpu.CompilerParams(vmem_limit_bytes=VMEM_LIMIT),
        cost_estimate=pl.CostEstimate(flops=1000, bytes_accessed=1000, transcendentals=0),
    )(out_grad, out_weight, out_grad, grad_mate)


def back_kernel(at_ref, mate_ref, *refs):
    me = at_ref[0]
    core, plane = me % 2, (me // 2) % 4
    got, outer, outs = refs[:PLACES], refs[PLACES : -PLACES - 1], refs[-PLACES - 1 :]
    total = outer[0][...]
    for ref in outer[1:]:
        total = total + ref[...]
    for j in range(PLACES):
        x = total
        for i in range(PLACES):
            if i != j:
                x = x + jnp.where((plane ^ i) < (plane ^ j), got[i][...], 0.0)
        outs[j][...] = x
        if j == 0:
            outs[-1][...] = x[2 * HEAD :] + jnp.where(core == 1, mate_ref[0, 2 * HEAD :, :], 0.0)


def early_kernel(at_ref, q_ref, nd_ref, gt_ref, z_ref, keep_ref, send_ref, inv_ref):
    def one(side, place, r, head, cols):
        fqs = split(feature(q_ref[:, cols].astype(F32)))
        denom = times_row(z_ref[pl.ds(head, 1), :], fqs, NT)
        inv = 1.0 / (nd_ref[head, HEAD : HEAD + 1, :] + denom)
        inv_ref[head] = first_of(inv)
        state = mm(split(gt_ref[head] * inv), fqs, NN)
        (keep_ref, send_ref)[side][place, pl.ds(r * HEAD, HEAD), :] = state

    each_head(at_ref, one)
    for place in range(PLACES):
        keep_ref[place, 2 * HEAD :, :] = jnp.zeros((HEADS, HEAD), F32)
        send_ref[place, 2 * HEAD :, :] = jnp.zeros((HEADS, HEAD), F32)


def attended_of(q_ref, nd_ref, inv_ref, s_ref, place, r, head, cols):
    state = s_ref[place, pl.ds(r * HEAD, HEAD), :]
    fqs = split(feature(q_ref[:, cols].astype(F32)))
    inv = inv_ref[head, :1, :]
    return (nd_ref[head, :HEAD, :] + mm(split(state), fqs, NT)) * inv, inv, fqs


def forward_kernel(at_ref, q_ref, nd_ref, inv_ref, s0_ref, s1_ref, keep_ref, send_ref):
    me = at_ref[0]
    core, chip = me % 2, me // 2

    def one(side, place, r, head, cols):
        att, _, _ = attended_of(q_ref, nd_ref, inv_ref, (s0_ref, s1_ref)[side], place, r, head, cols)
        low, high = att[:HALF], att[HALF:]
        keep_ref[head ^ chip] = jnp.where(core == 0, low, high)
        send_ref[head ^ chip] = jnp.where(core == 0, high, low)

    each_head(at_ref, one)


def denominator_kernel(at_ref, q_ref, nd_ref, gt_ref, inv_ref, s0_ref, s1_ref, dd_ref, dz_ref):
    def one(side, place, r, head, cols):
        att, inv, fqs = attended_of(q_ref, nd_ref, inv_ref, (s0_ref, s1_ref)[side], place, r, head, cols)
        dd = -jnp.sum(gt_ref[head] * att, axis=0, keepdims=True) * inv
        dd_ref[head] = first_of(dd)
        dz_ref[pl.ds(head, 1), :] = times_row(dd, fqs, NN)

    each_head(at_ref, one)


def backward_kernel(
    at_ref, q_ref, k_ref, v_ref, gt_ref, inv_ref, dd_ref, z_ref, s0_ref, s1_ref, qg_ref, dk_ref, dv_ref
):
    def one(side, place, r, head, cols):
        state = (s0_ref, s1_ref)[side][place, pl.ds(r * HEAD, HEAD), :]
        q, v = q_ref[:, cols].astype(F32), v_ref[:, cols]
        fq = feature(q)
        fqs, fks = split(fq), split(feature(k_ref[:, cols].astype(F32)))
        ss = split(masked(mm(fks, fqs, NT), 1))
        dn = split(gt_ref[head] * inv_ref[head, :1, :])
        dd = dd_ref[head, :1, :]
        ds = split(masked(mm((v,), dn, NN) + dd, 1))
        z = z_ref[pl.ds(head, 1), :]
        dd_rows, z_rows = (jnp.concatenate([first_of(x)] * 2, axis=0) for x in (dd, z))
        dfq = mm(ds, fks, TN) + mm(dn, split(state), TN) + 0.5 * mm(split(dd_rows), split(z_rows), TN)
        qg_ref[:, cols] = (dfq * slope(q, fq)).astype(BF16)
        dk_ref[:, cols] = mm(ds, fqs, NN)
        dv_ref[:, cols] = mm(ss, dn, NT)

    each_head(at_ref, one)


def finish_kernel(at_ref, k_ref, v_ref, dk_ref, dv_ref, dz_ref, s0_ref, s1_ref, kg_ref, vg_ref):
    def one(side, place, r, head, cols):
        states = split((s0_ref, s1_ref)[side][place, pl.ds(r * HEAD, HEAD), :])
        k = k_ref[:, cols].astype(F32)
        fk = feature(k)
        dfk = dk_ref[:, cols] + mm((v_ref[:, cols],), states, NN) + dz_ref[pl.ds(head, 1), :]
        kg_ref[:, cols] = (dfk * slope(k, fk)).astype(BF16)
        vg_ref[:, cols] = (dv_ref[:, cols] + mm(split(fk), states, NT)).astype(BF16)

    each_head(at_ref, one)


def weight_kernel(bit_set, a0_ref, a1_ref, g_ref, *refs):
    outs, a_ref = refs[:-1], refs[-1]
    t = a0_ref.shape[2]
    a_ref[:, :, :t] = a0_ref[...].astype(BF16)
    a_ref[:, :, t:] = a1_ref[...].astype(BF16)
    for out_ref, (start, width, order) in zip(outs, PARTS, strict=True):
        rels = [rel for rel in range(HEADS) if (rel >> order[0]) & 1 == bit_set]
        lhs = jnp.concatenate([a_ref[rel] for rel in rels], axis=0)
        for at in range(0, width, 256):
            got = jnp.dot(lhs, g_ref[:, start + at : start + at + 256], preferred_element_type=F32)
            out_ref[:, :, at : at + 256] = got.reshape(len(rels), HALF, 256)


def call(kernel, outs, *args, scratch=()):
    specs = [pl.BlockSpec(memory_space=pltpu.SMEM if a.size == 1 else pltpu.VMEM) for a in args]
    return pl.pallas_call(
        kernel,
        out_shape=tuple(outs),
        in_specs=specs,
        out_specs=tuple(pl.BlockSpec(memory_space=pltpu.VMEM) for _ in outs),
        scratch_shapes=list(scratch),
        compiler_params=pltpu.CompilerParams(vmem_limit_bytes=VMEM_LIMIT),
        cost_estimate=pl.CostEstimate(flops=1000, bytes_accessed=1000, transcendentals=0),
    )(*args)


def swap(x, mask):
    n = lax.axis_size("seq")
    return lax.ppermute(x, "seq", [(i, i ^ mask) for i in range(n)])


def after(first, *arrays):
    arrays, _ = lax.optimization_barrier((arrays, first))
    return arrays if len(arrays) > 1 else arrays[0]


def along(layer, later):
    n = lax.axis_size("seq")
    got = []
    for k in range(1, n // 8):
        pairs = [(i, i + 8 * k) for i in range(n - 8 * k)]
        got.append(lax.ppermute(layer, "seq", [(b, a) for a, b in pairs] if later else pairs))
    return got or [jnp.zeros_like(layer)]


def along_in_turn(layer, first, me, later, beside):
    outer, mask = jnp.zeros_like(layer), 8
    while mask < lax.axis_size("seq"):
        other = after(beside, first) if mask == 8 else swap(layer, mask)
        outer = outer + jnp.where(((me & mask) == 0) == later, other, 0.0)
        layer = layer + other
        mask *= 2
    return outer


def before(got, place, plane, later):
    out = 0.0
    for i, x in enumerate(got):
        if i != place:
            ahead = (plane ^ i) > (plane ^ place) if later else (plane ^ i) < (plane ^ place)
            out = out + jnp.where(ahead, x, 0.0)
    return out


def half(a, left, bit, which):
    return lax.index_in_dim(a.reshape((2,) * len(left) + a.shape[-2:]), which, left.index(bit), keepdims=False)


def one_turn(keep, got, left, bit):
    send = half(keep, left, bit, 1) + half(got, left, bit, 1)
    keep, got = after(send, keep, got)
    return half(keep, left, bit, 0) + half(got, left, bit, 0), swap(send, 2 << bit)


def sums_of(order, keep, got):
    left = sorted(order[1:], reverse=True)
    for bit in order[1:]:
        keep, got = one_turn(keep, got, left, bit)
        left = [b for b in left if b != bit]
        got = after((yield keep, got), got)


def body(queries, keys, values, out_weight, out_grad):
    t, model = out_grad.shape
    shape = jax.ShapeDtypeStruct
    me = lax.axis_index("seq")
    core, plane = me % 2, (me // 2) % 4
    at = me.astype(jnp.int32).reshape(1)
    packs = [shape((PLACES, PACK, HEAD), F32)] * 2
    row = shape((HEADS, 8, t), F32)
    sums = shape((HEADS, HEAD), F32)
    wide = shape((t, HEADS * HEAD), F32)
    narrow = shape((t, HEADS * HEAD), BF16)
    places = range(PLACES)
    own_sums = lambda x: x[2 * HEAD :]
    with_sums = lambda x, tail: jnp.concatenate([x[: 2 * HEAD], tail])

    keep, send = call(summary_kernel, packs, at, keys, values, scratch=(pltpu.VMEM((HEADS, HEAD), F32),))
    mate = swap(send, 1)
    grad_mate = swap(after(mate, out_grad).astype(F32), 1)
    (inner,) = call(
        inner_kernel, [shape((HEADS, ROWS, t), F32)], at, queries, keys, values
    )
    total = [keep[j] + mate[j] for j in places]
    got = [total[0]] + [swap(total[j], 2 * j) for j in places[1:]]
    layer, inner, grad_mate = lax.optimization_barrier((got[0] + got[1] + got[2] + got[3], inner, grad_mate))
    outer = along(layer, False)
    gt, grads = attended_grad(out_grad, out_weight, grad_mate)
    outer, gt, grads = lax.optimization_barrier((outer, gt, grads))
    pack = shape((PACK, HEAD), F32)
    *back, z_in = call(back_kernel, [pack] * PLACES + [sums], at, mate, *got, *outer)

    back = [swap(x, 2 * j) if j else x for j, x in enumerate(back)]
    dkeep, dsend, inv = call(early_kernel, packs + [row], at, queries, inner, gt, z_in)
    back, dsend = lax.optimization_barrier((back, dsend))
    dmate = swap(dsend, 1)
    s1 = swap(jnp.stack([x + jnp.where(core == 0, keep[j], 0.0) for j, x in enumerate(back)]), 1)
    s0 = jnp.stack([x + jnp.where(core == 1, mate[j], 0.0) for j, x in enumerate(back)])

    tall = shape((HEADS, HALF, t), F32)
    dtotal = [dkeep[j] + dmate[j] for j in places]
    dgot = [dtotal[0]] + [swap(dtotal[j], 2 * j) for j in places[1:]]
    a_keep, a_send = call(
        forward_kernel, [tall, tall], at, after(dtotal, queries), inner, inv, s0, s1
    )
    a_mate = swap(a_send, 1)

    weight = lambda bit: call(
        functools.partial(weight_kernel, bit),
        [shape((HEADS // 2, HALF, width), F32) for _, width, _ in PARTS],
        a_keep,
        a_mate,
        grads,
        scratch=(pltpu.VMEM((HEADS, HALF, 2 * t), BF16),),
    )
    sends, dgot = lax.optimization_barrier((list(weight(1)), dgot))
    a_mate = after(sends, a_mate)
    keeps = weight(0)
    gots = [swap(send, 2 << order[0]) for send, (_, _, order) in zip(sends, PARTS, strict=True)]
    dd, dz = call(
        denominator_kernel, [row, sums], at, after(sends, queries), inner, gt, inv, s0, s1
    )
    dlayer = with_sums(dgot[0] + dgot[1] + dgot[2] + dgot[3], dz)
    dfirst = swap(dlayer, 8)
    queries = after(dlayer, queries)
    query_grad, dk, dv = call(
        backward_kernel, [narrow, wide, wide], at, queries, keys, values, gt, inv, dd, z_in, s0, s1
    )
    douter = along_in_turn(dlayer, dfirst, me, True, dk)
    free = sums_of(PARTS[-1][2], keeps[-1], after(dk, gots[-1]))
    next(free)
    keeps, gots = keeps[:-1], gots[:-1]
    gots, douter = lax.optimization_barrier((gots, douter))
    dback = [douter + before(dgot, j, plane, True) for j in places]

    behind = own_sums(douter)
    lefts = [sorted(order[1:], reverse=True) for _, _, order in PARTS[:-1]]
    for turn in (1, 2):
        bits = [order[turn] for _, _, order in PARTS[:-1]]
        lists = list(zip(keeps, gots, lefts, bits, strict=True))
        sends = [half(k, left, bit, 1) + half(g, left, bit, 1) for k, g, left, bit in lists]
        keeps, gots = after(sends, keeps, gots)
        lists = list(zip(keeps, gots, lefts, bits, strict=True))
        keeps = [half(k, left, bit, 0) + half(g, left, bit, 0) for k, g, left, bit in lists]
        lefts = [[b for b in left if b != bit] for left, bit in zip(lefts, bits, strict=True)]
        gots = [swap(send, 2 << bit) for send, bit in zip(sends, bits, strict=True)]
        if turn == 2:
            free.send(sends)
            behind, dz_beside = behind + own_sums(across[0]), own_sums(across[1])
            up = jnp.stack([with_sums(dback[2], behind), with_sums(across[1], dz + dz_beside)])
            up = swap(after(sends, up), 4)
            dz_part = behind + own_sums(up[0]) + jnp.where((plane ^ 1) > plane, dz_beside, 0.0)
            dz_part = dz_part + jnp.where((plane ^ 2) > plane, own_sums(up[1]), 0.0)
            dback = [dback[0], across[0], up[0], up[1]]
            other = [x + jnp.where(core == 1, dkeep[j], 0.0) for j, x in enumerate(dback)]
            other = [with_sums(x, dz_part if j == 0 else dz) for j, x in enumerate(other)]
            other = jnp.stack(other)
            l1 = swap(other, 1)
            l0 = jnp.stack([x + jnp.where(core == 0, dmate[j], 0.0) for j, x in enumerate(dback)])
            result = free.send(other)
            ends = [one_turn(keeps[1], after(other, gots[1]), lefts[1], PARTS[1][2][3])]
        elif turn == 1:
            across = jnp.stack([with_sums(dback[1], behind), with_sums(dback[3], dz)])
            across = swap(after(sends, across), 2)
            gots, across = lax.optimization_barrier((gots, across))
    dz_in = dz_part + own_sums(l1[0]) + jnp.where(core == 0, own_sums(l1[1]), 0.0)
    key_grad, value_grad = call(finish_kernel, [narrow, narrow], at, keys, values, dk, dv, dz_in, l0, l1)
    ends.insert(0, one_turn(keeps[0], after(key_grad, gots[0]), lefts[0], PARTS[0][2][3]))
    key_grad, ends = lax.optimization_barrier((key_grad, [*ends, result]))
    parts = [keep_part + got for keep_part, got in ends]
    weight_grad = jnp.concatenate(parts, axis=1)
    return (query_grad, key_grad, value_grad, weight_grad)


def solution(mesh):
    placed = (
        P(("groups", "seq"), None),
        P(("groups", "seq"), None),
        P(("groups", "seq"), None),
        P(),
        P(("groups", "seq"), None),
    )
    return jax.shard_map(
        body,
        mesh=mesh,
        in_specs=placed,
        out_specs=(
            P(("groups", "seq"), None),
            P(("groups", "seq"), None),
            P(("groups", "seq"), None),
            P(("groups", "seq"), None),
        ),
        check_vma=False,
    )
```

```python
import functools

import jax
import jax.numpy as jnp
from jax import lax
from jax.experimental import pallas as pl
from jax.experimental.pallas import tpu as pltpu
from jax.sharding import PartitionSpec as P

HEADS = 16
HEAD = 128
HALF = HEAD // 2
ROWS = HEAD + 8
PACK = 2 * HEAD + HEADS
F32 = jnp.float32
BF16 = jnp.bfloat16
NN = (((1,), (0,)), ((), ()))
NT = (((1,), (1,)), ((), ()))
TN = (((0,), (0,)), ((), ()))
PARTS = ((0, 768, (1, 2, 3, 0)), (768, 768, (0, 1, 2, 3)), (1536, 512, (2, 0, 1, 3)))
PAIRS = HEADS // 2
PLACES = PAIRS // 2
VMEM_LIMIT = 12 * 1024 * 1024


def split(a):
    high = a.astype(BF16)
    return high, (a - high.astype(F32)).astype(BF16)


def mm(a, b, dims):
    out = lax.dot_general(a[0], b[0], dims, preferred_element_type=F32)
    if len(b) > 1:
        out = out + lax.dot_general(a[0], b[1], dims, preferred_element_type=F32)
    if len(a) > 1:
        out = out + lax.dot_general(a[1], b[0], dims, preferred_element_type=F32)
    return out


def feature(x):
    return jnp.where(x > 0, x + 1.0, jnp.exp(jnp.minimum(x, 0.0)))


def slope(x, f):
    return jnp.where(x > 0, 1.0, f)


def masked(a, query_dim):
    query = lax.broadcasted_iota(jnp.int32, a.shape, query_dim)
    return jnp.where(lax.broadcasted_iota(jnp.int32, a.shape, 1 - query_dim) <= query, a, 0.0)


def each_head(at_ref, one):
    me = at_ref[0]
    core, plane = me % 2, (me // 2) % 4

    def pair(turn, carry):
        place, r = turn // 2, turn % 2
        for side in range(2):
            head = (side ^ core) * 8 + (place ^ plane) * 2 + r
            one(side, place, r, head, pl.ds(pl.multiple_of(head * HEAD, HEAD), HEAD))
        return carry

    lax.fori_loop(0, HEADS // 2, pair, 0)


def first_of(row):
    return jnp.where(lax.broadcasted_iota(jnp.int32, (8, row.shape[1]), 0) == 0, row, 0.0)


def padded(row):
    return jnp.where(lax.broadcasted_iota(jnp.int32, (16, row.shape[1]), 0) == 0, row, 0.0)


def rows_of(r):
    return slice(r * HEAD, (r + 1) * HEAD)


def times_row(row, b, dims):
    high, low = split(row)
    width = row.shape[1]
    at_top = lax.broadcasted_iota(jnp.int32, (16, width), 0) < 8
    both = jnp.where(at_top, high.astype(F32), low.astype(F32)).astype(BF16)
    out = lax.dot_general(both, b[0], dims, preferred_element_type=F32)
    out = out[:1] + out[8:9]
    if len(b) > 1:
        out = out + lax.dot_general(both, b[1], dims, preferred_element_type=F32)[:1]
    return out


def summary_kernel(at_ref, k_ref, v_ref, keep_ref, send_ref, sum_ref):
    def one(side, place, r, head, cols):
        fk = feature(k_ref[:, cols].astype(F32))
        state = mm((v_ref[:, cols],), split(fk), TN)
        (keep_ref, send_ref)[side][place, pl.ds(r * HEAD, HEAD), :] = state
        sum_ref[pl.ds(head, 1), :] = jnp.sum(fk, axis=0, keepdims=True)

    each_head(at_ref, one)
    for place in range(PLACES):
        keep_ref[place, 2 * HEAD :, :] = sum_ref[...]
        send_ref[place, 2 * HEAD :, :] = sum_ref[...]


def inner_kernel(at_ref, q_ref, k_ref, v_ref, nd_ref):
    def one(side, place, r, head, cols):
        fqs, fks = split(feature(q_ref[:, cols].astype(F32))), split(feature(k_ref[:, cols].astype(F32)))
        scores = masked(mm(fks, fqs, NT), 1)
        nd_ref[head, :HEAD, :] = mm((v_ref[:, cols],), split(scores), TN)
        nd_ref[head, HEAD:, :] = first_of(jnp.sum(scores, axis=0, keepdims=True))

    each_head(at_ref, one)


def grad_kernel(g_ref, w_ref, own_ref, mate_ref, gt_ref, both_ref):
    got = lax.dot_general(w_ref[...], g_ref[...], NT, preferred_element_type=F32)
    gt_ref[...] = got.reshape(gt_ref.shape)
    t = g_ref.shape[0]
    both_ref[:t, :] = own_ref[...]
    both_ref[t:, :] = mate_ref[...].astype(BF16)


def attended_grad(out_grad, out_weight, grad_mate):
    t, model = out_grad.shape
    some = 4
    steps = HEADS // some
    columns = lambda rows: pl.BlockSpec((rows, model // steps), lambda i: (0, i))
    return pl.pallas_call(
        grad_kernel,
        grid=(steps,),
        out_shape=(
            jax.ShapeDtypeStruct((HEADS, HEAD, t), F32),
            jax.ShapeDtypeStruct((2 * t, model), BF16),
        ),
        in_specs=[
            pl.BlockSpec((t, model), lambda i: (0, 0)),
            pl.BlockSpec((some * HEAD, model), lambda i: (i, 0)),
            columns(t),
            columns(t),
        ],
        out_specs=(pl.BlockSpec((some, HEAD, t), lambda i: (i, 0, 0)), columns(2 * t)),
        compiler_params=pltpu.CompilerParams(vmem_limit_bytes=VMEM_LIMIT),
        cost_estimate=pl.CostEstimate(flops=1000, bytes_accessed=1000, transcendentals=0),
    )(out_grad, out_weight, out_grad, grad_mate)


def back_kernel(at_ref, mate_ref, *refs):
    me = at_ref[0]
    core, plane = me % 2, (me // 2) % 4
    got, outer, outs = refs[:PLACES], refs[PLACES : -PLACES - 1], refs[-PLACES - 1 :]
    total = outer[0][...]
    for ref in outer[1:]:
        total = total + ref[...]
    for j in range(PLACES):
        x = total
        for i in range(PLACES):
            if i != j:
                x = x + jnp.where((plane ^ i) < (plane ^ j), got[i][...], 0.0)
        outs[j][...] = x
        if j == 0:
            outs[-1][...] = x[2 * HEAD :] + jnp.where(core == 1, mate_ref[0, 2 * HEAD :, :], 0.0)


def early_kernel(at_ref, q_ref, nd_ref, gt_ref, z_ref, keep_ref, send_ref, inv_ref):
    def one(side, place, r, head, cols):
        fqs = split(feature(q_ref[:, cols].astype(F32)))
        denom = times_row(z_ref[pl.ds(head, 1), :], fqs, NT)
        inv = 1.0 / (nd_ref[head, HEAD : HEAD + 1, :] + denom)
        inv_ref[head] = first_of(inv)
        state = mm(split(gt_ref[head] * inv), fqs, NN)
        (keep_ref, send_ref)[side][place, pl.ds(r * HEAD, HEAD), :] = state

    each_head(at_ref, one)
    for place in range(PLACES):
        keep_ref[place, 2 * HEAD :, :] = jnp.zeros((HEADS, HEAD), F32)
        send_ref[place, 2 * HEAD :, :] = jnp.zeros((HEADS, HEAD), F32)


def attended_of(q_ref, nd_ref, inv_ref, s_ref, place, r, head, cols):
    state = s_ref[place, pl.ds(r * HEAD, HEAD), :]
    fqs = split(feature(q_ref[:, cols].astype(F32)))
    inv = inv_ref[head, :1, :]
    return (nd_ref[head, :HEAD, :] + mm(split(state), fqs, NT)) * inv, inv, fqs


def forward_kernel(at_ref, q_ref, nd_ref, inv_ref, s0_ref, s1_ref, keep_ref, send_ref):
    me = at_ref[0]
    core, chip = me % 2, me // 2

    def one(side, place, r, head, cols):
        att, _, _ = attended_of(q_ref, nd_ref, inv_ref, (s0_ref, s1_ref)[side], place, r, head, cols)
        low, high = att[:HALF], att[HALF:]
        keep_ref[head ^ chip] = jnp.where(core == 0, low, high)
        send_ref[head ^ chip] = jnp.where(core == 0, high, low)

    each_head(at_ref, one)


def denominator_kernel(at_ref, q_ref, nd_ref, gt_ref, inv_ref, s0_ref, s1_ref, dd_ref, dz_ref):
    def one(side, place, r, head, cols):
        att, inv, fqs = attended_of(q_ref, nd_ref, inv_ref, (s0_ref, s1_ref)[side], place, r, head, cols)
        dd = -jnp.sum(gt_ref[head] * att, axis=0, keepdims=True) * inv
        dd_ref[head] = first_of(dd)
        dz_ref[pl.ds(head, 1), :] = times_row(dd, fqs, NN)

    each_head(at_ref, one)


def backward_kernel(
    at_ref, q_ref, k_ref, v_ref, gt_ref, inv_ref, dd_ref, z_ref, s0_ref, s1_ref, qg_ref, dk_ref, dv_ref
):
    def one(side, place, r, head, cols):
        state = (s0_ref, s1_ref)[side][place, pl.ds(r * HEAD, HEAD), :]
        q, v = q_ref[:, cols].astype(F32), v_ref[:, cols]
        fq = feature(q)
        fqs, fks = split(fq), split(feature(k_ref[:, cols].astype(F32)))
        ss = split(masked(mm(fks, fqs, NT), 1))
        dd = dd_ref[head, :1, :]
        dn_dd = split(jnp.concatenate([gt_ref[head] * inv_ref[head, :1, :], padded(dd)], axis=0))
        dn = tuple(x[:HEAD] for x in dn_dd)
        ds = split(masked(mm((v,), dn, NN) + dd, 1))
        z = z_ref[pl.ds(head, 1), :]
        state_z = split(jnp.concatenate([state, padded(z)], axis=0))
        dfq = mm(ds, fks, TN) + mm(dn_dd, state_z, TN)
        qg_ref[:, cols] = (dfq * slope(q, fq)).astype(BF16)
        dk_ref[:, cols] = mm(ds, fqs, NN)
        dv_ref[:, cols] = mm(ss, dn, NT)

    each_head(at_ref, one)


def finish_kernel(at_ref, k_ref, v_ref, dk_ref, dv_ref, dz_ref, s0_ref, s1_ref, kg_ref, vg_ref):
    def one(side, place, r, head, cols):
        states = split((s0_ref, s1_ref)[side][place, pl.ds(r * HEAD, HEAD), :])
        k = k_ref[:, cols].astype(F32)
        fk = feature(k)
        dfk = dk_ref[:, cols] + mm((v_ref[:, cols],), states, NN) + dz_ref[pl.ds(head, 1), :]
        kg_ref[:, cols] = (dfk * slope(k, fk)).astype(BF16)
        vg_ref[:, cols] = (dv_ref[:, cols] + mm(split(fk), states, NT)).astype(BF16)

    each_head(at_ref, one)


def weight_kernel(bit_set, a0_ref, a1_ref, g_ref, *refs):
    outs, a_ref = refs[:-1], refs[-1]
    t = a0_ref.shape[2]
    a_ref[:, :, :t] = a0_ref[...].astype(BF16)
    a_ref[:, :, t:] = a1_ref[...].astype(BF16)
    for out_ref, (start, width, order) in zip(outs, PARTS, strict=True):
        rels = [rel for rel in range(HEADS) if (rel >> order[0]) & 1 == bit_set]
        lhs = jnp.concatenate([a_ref[rel] for rel in rels], axis=0)
        for at in range(0, width, 256):
            got = jnp.dot(lhs, g_ref[:, start + at : start + at + 256], preferred_element_type=F32)
            out_ref[:, :, at : at + 256] = got.reshape(len(rels), HALF, 256)


def call(kernel, outs, *args, scratch=()):
    specs = [pl.BlockSpec(memory_space=pltpu.SMEM if a.size == 1 else pltpu.VMEM) for a in args]
    return pl.pallas_call(
        kernel,
        out_shape=tuple(outs),
        in_specs=specs,
        out_specs=tuple(pl.BlockSpec(memory_space=pltpu.VMEM) for _ in outs),
        scratch_shapes=list(scratch),
        compiler_params=pltpu.CompilerParams(vmem_limit_bytes=VMEM_LIMIT),
        cost_estimate=pl.CostEstimate(flops=1000, bytes_accessed=1000, transcendentals=0),
    )(*args)


def swap(x, mask):
    n = lax.axis_size("seq")
    return lax.ppermute(x, "seq", [(i, i ^ mask) for i in range(n)])


def after(first, *arrays):
    arrays, _ = lax.optimization_barrier((arrays, first))
    return arrays if len(arrays) > 1 else arrays[0]


def along(layer, later):
    n = lax.axis_size("seq")
    got = []
    for k in range(1, n // 8):
        pairs = [(i, i + 8 * k) for i in range(n - 8 * k)]
        got.append(lax.ppermute(layer, "seq", [(b, a) for a, b in pairs] if later else pairs))
    return got or [jnp.zeros_like(layer)]


def along_in_turn(layer, first, me, later, beside):
    outer, mask = jnp.zeros_like(layer), 8
    while mask < lax.axis_size("seq"):
        other = after(beside, first) if mask == 8 else swap(layer, mask)
        outer = outer + jnp.where(((me & mask) == 0) == later, other, 0.0)
        layer = layer + other
        mask *= 2
    return outer


def before(got, place, plane, later):
    out = 0.0
    for i, x in enumerate(got):
        if i != place:
            ahead = (plane ^ i) > (plane ^ place) if later else (plane ^ i) < (plane ^ place)
            out = out + jnp.where(ahead, x, 0.0)
    return out


def half(a, left, bit, which):
    return lax.index_in_dim(a.reshape((2,) * len(left) + a.shape[-2:]), which, left.index(bit), keepdims=False)


def one_turn(keep, got, left, bit):
    send = half(keep, left, bit, 1) + half(got, left, bit, 1)
    keep, got = after(send, keep, got)
    return half(keep, left, bit, 0) + half(got, left, bit, 0), swap(send, 2 << bit)


def sums_of(order, keep, got):
    left = sorted(order[1:], reverse=True)
    for bit in order[1:]:
        keep, got = one_turn(keep, got, left, bit)
        left = [b for b in left if b != bit]
        got = after((yield keep, got), got)


def body(queries, keys, values, out_weight, out_grad):
    t, model = out_grad.shape
    shape = jax.ShapeDtypeStruct
    me = lax.axis_index("seq")
    core, plane = me % 2, (me // 2) % 4
    at = me.astype(jnp.int32).reshape(1)
    packs = [shape((PLACES, PACK, HEAD), F32)] * 2
    row = shape((HEADS, 8, t), F32)
    sums = shape((HEADS, HEAD), F32)
    wide = shape((t, HEADS * HEAD), F32)
    narrow = shape((t, HEADS * HEAD), BF16)
    places = range(PLACES)
    own_sums = lambda x: x[2 * HEAD :]
    with_sums = lambda x, tail: jnp.concatenate([x[: 2 * HEAD], tail])

    keep, send = call(summary_kernel, packs, at, keys, values, scratch=(pltpu.VMEM((HEADS, HEAD), F32),))
    mate = swap(send, 1)
    grad_mate = swap(after(mate, out_grad).astype(F32), 1)
    (inner,) = call(
        inner_kernel, [shape((HEADS, ROWS, t), F32)], at, queries, keys, values
    )
    total = [keep[j] + mate[j] for j in places]
    got = [total[0]] + [swap(total[j], 2 * j) for j in places[1:]]
    layer, inner, grad_mate = lax.optimization_barrier((got[0] + got[1] + got[2] + got[3], inner, grad_mate))
    outer = along(layer, False)
    gt, grads = attended_grad(out_grad, out_weight, grad_mate)
    outer, gt, grads = lax.optimization_barrier((outer, gt, grads))
    pack = shape((PACK, HEAD), F32)
    *back, z_in = call(back_kernel, [pack] * PLACES + [sums], at, mate, *got, *outer)

    back = [swap(x, 2 * j) if j else x for j, x in enumerate(back)]
    dkeep, dsend, inv = call(early_kernel, packs + [row], at, queries, inner, gt, z_in)
    back, dsend = lax.optimization_barrier((back, dsend))
    dmate = swap(dsend, 1)
    s1 = swap(jnp.stack([x + jnp.where(core == 0, keep[j], 0.0) for j, x in enumerate(back)]), 1)
    s0 = jnp.stack([x + jnp.where(core == 1, mate[j], 0.0) for j, x in enumerate(back)])

    tall = shape((HEADS, HALF, t), F32)
    dtotal = [dkeep[j] + dmate[j] for j in places]
    dgot = [dtotal[0]] + [swap(dtotal[j], 2 * j) for j in places[1:]]
    a_keep, a_send = call(
        forward_kernel, [tall, tall], at, after(dtotal, queries), inner, inv, s0, s1
    )
    a_mate = swap(a_send, 1)

    weight = lambda bit: call(
        functools.partial(weight_kernel, bit),
        [shape((HEADS // 2, HALF, width), F32) for _, width, _ in PARTS],
        a_keep,
        a_mate,
        grads,
        scratch=(pltpu.VMEM((HEADS, HALF, 2 * t), BF16),),
    )
    sends, dgot = lax.optimization_barrier((list(weight(1)), dgot))
    a_mate = after(sends, a_mate)
    keeps = weight(0)
    gots = [swap(send, 2 << order[0]) for send, (_, _, order) in zip(sends, PARTS, strict=True)]
    dd, dz = call(
        denominator_kernel, [row, sums], at, after(sends, queries), inner, gt, inv, s0, s1
    )
    dlayer = with_sums(dgot[0] + dgot[1] + dgot[2] + dgot[3], dz)
    dfirst = swap(dlayer, 8)
    queries = after(dlayer, queries)
    query_grad, dk, dv = call(
        backward_kernel, [narrow, wide, wide], at, queries, keys, values, gt, inv, dd, z_in, s0, s1
    )
    douter = along_in_turn(dlayer, dfirst, me, True, dk)
    free = sums_of(PARTS[-1][2], keeps[-1], after(dk, gots[-1]))
    next(free)
    keeps, gots = keeps[:-1], gots[:-1]
    gots, douter = lax.optimization_barrier((gots, douter))
    dback = [douter + before(dgot, j, plane, True) for j in places]

    behind = own_sums(douter)
    lefts = [sorted(order[1:], reverse=True) for _, _, order in PARTS[:-1]]
    for turn in (1, 2):
        bits = [order[turn] for _, _, order in PARTS[:-1]]
        lists = list(zip(keeps, gots, lefts, bits, strict=True))
        sends = [half(k, left, bit, 1) + half(g, left, bit, 1) for k, g, left, bit in lists]
        keeps, gots = after(sends, keeps, gots)
        lists = list(zip(keeps, gots, lefts, bits, strict=True))
        keeps = [half(k, left, bit, 0) + half(g, left, bit, 0) for k, g, left, bit in lists]
        lefts = [[b for b in left if b != bit] for left, bit in zip(lefts, bits, strict=True)]
        gots = [swap(send, 2 << bit) for send, bit in zip(sends, bits, strict=True)]
        if turn == 2:
            free.send(sends)
            behind, dz_beside = behind + own_sums(across[0]), own_sums(across[1])
            up = jnp.stack([with_sums(dback[2], behind), with_sums(across[1], dz + dz_beside)])
            up = swap(after(sends, up), 4)
            dz_part = behind + own_sums(up[0]) + jnp.where((plane ^ 1) > plane, dz_beside, 0.0)
            dz_part = dz_part + jnp.where((plane ^ 2) > plane, own_sums(up[1]), 0.0)
            dback = [dback[0], across[0], up[0], up[1]]
            other = [x + jnp.where(core == 1, dkeep[j], 0.0) for j, x in enumerate(dback)]
            other = [with_sums(x, dz_part if j == 0 else dz) for j, x in enumerate(other)]
            other = jnp.stack(other)
            l1 = swap(other, 1)
            l0 = jnp.stack([x + jnp.where(core == 0, dmate[j], 0.0) for j, x in enumerate(dback)])
            result = free.send(other)
            ends = [one_turn(keeps[1], after(other, gots[1]), lefts[1], PARTS[1][2][3])]
        elif turn == 1:
            across = jnp.stack([with_sums(dback[1], behind), with_sums(dback[3], dz)])
            across = swap(after(sends, across), 2)
            gots, across = lax.optimization_barrier((gots, across))
    dz_in = dz_part + own_sums(l1[0]) + jnp.where(core == 0, own_sums(l1[1]), 0.0)
    key_grad, value_grad = call(finish_kernel, [narrow, narrow], at, keys, values, dk, dv, dz_in, l0, l1)
    ends.insert(0, one_turn(keeps[0], after(key_grad, gots[0]), lefts[0], PARTS[0][2][3]))
    key_grad, ends = lax.optimization_barrier((key_grad, [*ends, result]))
    parts = [keep_part + got for keep_part, got in ends]
    weight_grad = jnp.concatenate(parts, axis=1)
    return (query_grad, key_grad, value_grad, weight_grad)


def solution(mesh):
    placed = (
        P(("groups", "seq"), None),
        P(("groups", "seq"), None),
        P(("groups", "seq"), None),
        P(),
        P(("groups", "seq"), None),
    )
    return jax.shard_map(
        body,
        mesh=mesh,
        in_specs=placed,
        out_specs=(
            P(("groups", "seq"), None),
            P(("groups", "seq"), None),
            P(("groups", "seq"), None),
            P(("groups", "seq"), None),
        ),
        check_vma=False,
    )
```
